256 devices in a mesh: dom: 256 (over z, y, x, core).
Axes of the slice: x: 4, y: 4, z: 8, core: 2. Of those that a mesh axis runs over, the one named last changes fastest.
Arguments:
- fwd_dofs: float32 [35, 9, 65536], P(None, None, 'dom'), may hold values from -6 to 6
- adj_dofs: float32 [35, 9, 65536], P(None, None, 'dom'), may hold values from -6 to 6
- star: float32 [3, 9, 9, 65536], P(None, None, None, 'dom'), may hold values from -4 to 4
- flux_local: float32 [4, 9, 9, 65536], P(None, None, None, 'dom'), may hold values from -2 to 2
- flux_neighbor: float32 [4, 9, 9, 65536], P(None, None, None, 'dom'), may hold values from -2 to 2
- timescale: float32 [65536], P('dom'), may hold values from 0.6 to 4.05
- cluster: int32 [65536], P('dom'), may hold values from 0 to 3, as said below
- face_kind: int32 [4, 65536], P(None, 'dom'), may hold values from 0 to 3, as said below
- neighbor_index: int32 [4, 65536], P(None, 'dom'), may hold values from 0 to 255, as said below
- neighbor_face: int32 [4, 65536], P(None, 'dom'), may hold values from 0 to 3, as said below
- orientation: int32 [4, 65536], P(None, 'dom'), may hold values from 0 to 2
- send_element: int32 [4, 16384], P(None, 'dom'), may hold values from 0 to 255, as said below
- send_face: int32 [4, 16384], P(None, 'dom'), may hold values from 0 to 3, as said below
- stiffness: float32 [3, 35, 35], replicated, may hold values from -1 to 1
- face_proj: float32 [4, 15, 35], replicated, may hold values from -1 to 1
- face_lift: float32 [4, 35, 15], replicated, may hold values from -1.5 to 1.5
- face_orient: float32 [3, 15, 15], replicated, may hold values from -1.5 to 1.5
Outputs:
- fwd_final: float32 [35, 9, 65536], P(None, None, 'dom')
- adj_final: float32 [35, 9, 65536], P(None, None, 'dom')
- sensitivity: float32 [65536], P('dom')
The draws below stay inside these ranges and needn't reach their ends.
Inputs may be any that keep to these rules, and one draw needn't show every extreme that they name: At most 64 elements of one partition (one block of 256 consecutive entries) are in cluster 0, and some partition has exactly 64. `face_kind`: 0: neighbour in the same partition; 1: neighbour in another partition; 2: free surface; 3: absorbing boundary. A partition has exactly 64 faces of kind 1 toward each partition whose index differs by 1 or 2, when it exists. `neighbor_index`: kind 0: the neighbour's element in the partition, and that face names this element and face back. Kind 1: a receive slot g * 64 + j, the partition at index offset (-2, -1, 1, 2)[g] exists, and every such slot is named by exactly one face. Unused for kinds 2 and 3. `neighbor_face`: for kind 1 it equals the send_face entry of the slot that the face names. `send_element`: group g of a partition holds, slot by slot, its elements whose data go to the partition at index offset (2, 1, -1, -2)[g]; that partition names slot j of group g in its neighbor_index. Entries toward missing partitions are unused. `send_face`: the face of each send slot; the pair of element and face shares that face with the receiving element.
All inputs are finite; a program needn't handle non-finite values.
Results may differ from the reference program's by a relative error of at most 0.0003.
Values sent between devices are 32-bit elements; how exact they have to be, the bound alone decides.
No kernel may reach another device: no remote copies, remote signals or barrier semaphores. Data moves between devices by JAX's collectives and lax.ppermute only.
A program may use at most 128 MiB of HBM per device.

```python
import math
import jax
import jax.numpy as jnp
from jax import lax

ELEMENTS = 256
BASIS = 35
FACE_BASIS = 15
QUANT = 9
ORDER = 5
SLOTS = 64
BOUNDARY = 32
FINE_MAX = 64
PARTITIONS = 256
ELEMENTS_ALL = 65536


def mesh_tables(key):
    pieces = PARTITIONS
    per_part = ELEMENTS
    slot_count = SLOTS
    face_count = 4 * per_part
    subkeys = jax.random.split(key, pieces)
    shuffled = jax.vmap(lambda subkey: jax.random.permutation(subkey, face_count))(subkeys).astype(jnp.int32)
    surface = jax.random.randint(jax.random.fold_in(key, 101), (pieces, face_count), 2, 4).astype(jnp.int32)
    kind_table = jnp.zeros((pieces, face_count), jnp.int32)
    index_table = jnp.zeros((pieces, face_count), jnp.int32)
    face_table = jnp.zeros((pieces, face_count), jnp.int32)
    row_ids = jnp.arange(pieces, dtype=jnp.int32)[:, None]
    places = jnp.arange(slot_count, dtype=jnp.int32)[None, :]
    sender_elems = []
    sender_sides = []
    for group_index, offset in enumerate((-2, -1, 1, 2)):
        own_faces = shuffled[:, group_index * slot_count:(group_index + 1) * slot_count]
        partner_id = jnp.arange(pieces, dtype=jnp.int32) + offset
        present = ((partner_id >= 0) & (partner_id < pieces))[:, None]
        partner = shuffled[jnp.clip(partner_id, 0, pieces - 1), (3 - group_index) * slot_count:(4 - group_index) * slot_count]
        kind_table = kind_table.at[row_ids, own_faces].set(jnp.where(present, 1, surface[row_ids, own_faces]).astype(jnp.int32))
        index_table = index_table.at[row_ids, own_faces].set(jnp.where(present, group_index * slot_count + places, 0).astype(jnp.int32))
        face_table = face_table.at[row_ids, own_faces].set(jnp.where(present, partner // per_part, own_faces // per_part).astype(jnp.int32))
        sender_elems.insert(0, own_faces % per_part)
        sender_sides.insert(0, own_faces // per_part)
    border_faces = shuffled[:, 4 * slot_count:4 * slot_count + BOUNDARY]
    kind_table = kind_table.at[row_ids, border_faces].set(surface[row_ids, border_faces])
    face_table = face_table.at[row_ids, border_faces].set(border_faces // per_part)
    paired = shuffled[:, 4 * slot_count + BOUNDARY:]
    left_faces = paired[:, 0::2]
    right_faces = paired[:, 1::2]
    kind_table = kind_table.at[row_ids, left_faces].set(0).at[row_ids, right_faces].set(0)
    index_table = index_table.at[row_ids, left_faces].set(right_faces % per_part).at[row_ids, right_faces].set(left_faces % per_part)
    face_table = face_table.at[row_ids, left_faces].set(right_faces // per_part).at[row_ids, right_faces].set(left_faces // per_part)

    def layout(table):
        return table.reshape(pieces, 4, per_part).transpose(1, 0, 2).reshape(4, pieces * per_part)
    send_elems = jnp.stack(sender_elems).reshape(4, pieces * slot_count).astype(jnp.int32)
    send_sides = jnp.stack(sender_sides).reshape(4, pieces * slot_count).astype(jnp.int32)
    return (layout(kind_table), layout(index_table), layout(face_table), send_elems, send_sides)


def draw_face_kind(key, part):
    tables = mesh_tables(key)
    return tables[0]


def draw_neighbor_index(key, part):
    tables = mesh_tables(key)
    return tables[1]


def draw_neighbor_face(key, part):
    tables = mesh_tables(key)
    return tables[2]


def draw_send_element(key, part):
    tables = mesh_tables(key)
    return tables[3]


def draw_send_face(key, part):
    tables = mesh_tables(key)
    return tables[4]


def draw_cluster(key, part):
    key = jax.random.fold_in(key, 3)
    first_key, second_key, third_key, fourth_key = jax.random.split(key, 4)
    lowest = max(FINE_MAX // 8, 1)
    counts = jax.random.randint(first_key, (PARTITIONS,), lowest, FINE_MAX + 1)
    busiest = jax.random.randint(second_key, (), 0, PARTITIONS)
    counts = counts.at[busiest].set(FINE_MAX)
    ranking = jax.vmap(lambda subkey: jax.random.permutation(subkey, ELEMENTS))(jax.random.split(third_key, PARTITIONS))
    coarse = jax.random.randint(fourth_key, (PARTITIONS, ELEMENTS), 1, 4)
    return jnp.where(ranking < counts[:, None], 0, coarse).astype(jnp.int32).reshape(PARTITIONS * ELEMENTS)


def draw_timescale(key, part):
    key = jax.random.fold_in(key, 7)
    first_key, second_key, third_key = jax.random.split(key, 3)
    common = jnp.exp(jax.random.uniform(first_key, (), jnp.float32, jnp.log(0.6), jnp.log(0.9)))
    partition = jnp.exp(jax.random.uniform(second_key, (PARTITIONS, 1), jnp.float32, 0.0, jnp.log(3.0)))
    element = jnp.exp(jax.random.uniform(third_key, (PARTITIONS, ELEMENTS), jnp.float32, 0.0, jnp.log(1.5)))
    return (common * partition * element).reshape(PARTITIONS * ELEMENTS)


def set_ends(values, rng, low, high):
    shape = values.shape
    spot = [jax.random.randint(jax.random.fold_in(rng, axis), (), 0, shape[axis]) for axis in range(len(shape))]
    values = values.at[tuple(spot)].set(low)
    longest = shape.index(max(shape))
    spot[longest] = (spot[longest] + 1) % shape[longest]
    return values.at[tuple(spot)].set(high)


def steps_of(rng, shape, cuts, smallest, largest):
    factor_of = 1.0
    for dim, shards_of in cuts:
        draws = jax.random.uniform(jax.random.fold_in(jax.random.fold_in(rng, 6), dim), (shards_of,), jnp.float32, smallest / len(cuts), largest / len(cuts))
        factor_of = factor_of * jnp.repeat(jnp.exp(draws), shape[dim] // shards_of).reshape((-1,) + (1,) * (len(shape) - 1 - dim))
    return factor_of


def scatter_about(rng, shape, scale, limit, cuts=(), kind=jnp.bfloat16):
    result = scale * jax.random.normal(rng, shape, jnp.float32)
    if cuts:
        result = result * steps_of(rng, shape, cuts, -0.22, 0.18)
    return jnp.clip(result, -limit, limit).astype(kind)


def setup_inputs(seed: int = 0) -> dict:
    key_of = jax.random.split(jax.random.key(seed), 18)
    fwd_dofs = scatter_about(key_of[0], (BASIS, QUANT, ELEMENTS_ALL), 1.0, 6.0, ((2, 256),), jnp.float32)
    adj_dofs = scatter_about(key_of[1], (BASIS, QUANT, ELEMENTS_ALL), 1.0, 6.0, ((2, 256),), jnp.float32)
    star = scatter_about(key_of[2], (3, QUANT, QUANT, ELEMENTS_ALL), 0.5, 4.0, ((3, 256),), jnp.float32)
    flux_local = scatter_about(key_of[3], (4, QUANT, QUANT, ELEMENTS_ALL), QUANT ** -0.5, 2.0, ((3, 256),), jnp.float32)
    flux_neighbor = scatter_about(key_of[4], (4, QUANT, QUANT, ELEMENTS_ALL), QUANT ** -0.5, 2.0, ((3, 256),), jnp.float32)
    timescale = draw_timescale(jax.random.fold_in(key_of[17], 71), 0)
    cluster = draw_cluster(jax.random.fold_in(key_of[17], 71), 0)
    face_kind = draw_face_kind(jax.random.fold_in(key_of[17], 71), 0)
    neighbor_index = draw_neighbor_index(jax.random.fold_in(key_of[17], 71), 0)
    neighbor_face = draw_neighbor_face(jax.random.fold_in(key_of[17], 71), 0)
    orientation = set_ends(jax.random.randint(key_of[10], (4, ELEMENTS_ALL), 0, 3), jax.random.fold_in(key_of[10], 1), 0, 2).astype(jnp.int32)
    send_element = draw_send_element(jax.random.fold_in(key_of[17], 71), 0)
    send_face = draw_send_face(jax.random.fold_in(key_of[17], 71), 0)
    stiffness = scatter_about(key_of[13], (3, BASIS, BASIS), BASIS ** -0.5, 1.0, (), jnp.float32)
    face_proj = scatter_about(key_of[14], (4, FACE_BASIS, BASIS), BASIS ** -0.5, 1.0, (), jnp.float32)
    face_lift = scatter_about(key_of[15], (4, BASIS, FACE_BASIS), FACE_BASIS ** -0.5, 1.5, (), jnp.float32)
    face_orient = scatter_about(key_of[16], (3, FACE_BASIS, FACE_BASIS), FACE_BASIS ** -0.5, 1.5, (), jnp.float32)
    return {"fwd_dofs": fwd_dofs, "adj_dofs": adj_dofs, "star": star, "flux_local": flux_local, "flux_neighbor": flux_neighbor, "timescale": timescale, "cluster": cluster, "face_kind": face_kind, "neighbor_index": neighbor_index, "neighbor_face": neighbor_face, "orientation": orientation, "send_element": send_element, "send_face": send_face, "stiffness": stiffness, "face_proj": face_proj, "face_lift": face_lift, "face_orient": face_orient}


highest = lax.Precision.HIGHEST
MIRROR = (-1.0, 1.0, 1.0, -1.0, 1.0, -1.0, 1.0, 1.0, 1.0)
OFFSETS = (-2, -1, 1, 2)


def by_partition(values, pieces):
    shaped = values.reshape(values.shape[:-1] + (pieces, values.shape[-1] // pieces))
    return jnp.moveaxis(shaped, -2, 0)


def from_partition(values):
    rolled = jnp.moveaxis(values, 0, -2)
    return rolled.reshape(rolled.shape[:-2] + (rolled.shape[-2] * rolled.shape[-1],))


def apply_star(fields, matrices, stiff_mats):
    spread = jnp.einsum('dab,nbpe->ndape', stiff_mats, fields, precision=highest)
    forward = jnp.einsum('dape,dqpe->aqe', spread[0], matrices, precision=highest)
    adjoint = jnp.einsum('dape,dpqe->aqe', spread[1], matrices, precision=highest)
    return jnp.stack([forward, adjoint])


def expansion(fields, matrices, stiffness):
    series = [fields]
    for degree in range(ORDER - 1):
        series.append(apply_star(series[-1], matrices, stiffness))
    return series


def integral(series, start_time, end_time):
    summed = jnp.zeros_like(series[0])
    for degree in range(ORDER):
        weight = (end_time ** (degree + 1) - start_time ** (degree + 1)) / math.factorial(degree + 1)
        summed = summed + weight * series[degree]
    return summed


def face_values(integrals, face_proj):
    return jnp.einsum('fba,naqe->nbqfe', face_proj, integrals, precision=highest)


def face_update(integrals, own_faces, gathered, face_kind, orientation, flux_local, flux_neighbor, face_orient, face_lift, stiffness, star):
    selector = (orientation[None] == jnp.arange(3, dtype=jnp.int32)[:, None, None]).astype(jnp.float32)
    candidates = jnp.einsum('obc,ncqfe->onbqfe', face_orient, gathered, precision=highest)
    oriented = jnp.sum(candidates * selector[:, None, None, None], axis=0)
    mirror = jnp.array(MIRROR, jnp.float32)[None, None, :, None, None]
    linked = (face_kind <= 1)[None, None, None]
    surface = (face_kind == 2)[None, None, None]
    neighbor = jnp.where(linked, oriented, jnp.where(surface, own_faces * mirror, 0.0))
    forward_terms = jnp.einsum('bpfe,fqpe->bqfe', own_faces[0], flux_local, precision=highest) + jnp.einsum('bpfe,fqpe->bqfe', neighbor[0], flux_neighbor, precision=highest)
    adjoint_terms = jnp.einsum('bpfe,fpqe->bqfe', own_faces[1], flux_local, precision=highest) + jnp.einsum('bpfe,fpqe->bqfe', neighbor[1], flux_neighbor, precision=highest)
    lifted = jnp.einsum('fab,nbqfe->naqe', face_lift, jnp.stack([forward_terms, adjoint_terms]), precision=highest)
    volume = apply_star(integrals, star, jnp.swapaxes(stiffness, 1, 2))
    return volume + lifted


def reference(fwd_dofs, adj_dofs, star, flux_local, flux_neighbor, timescale, cluster, face_kind, neighbor_index, neighbor_face, orientation, send_element, send_face, stiffness, face_proj, face_lift, face_orient):
    pieces = PARTITIONS
    fields = by_partition(jnp.stack([fwd_dofs, adj_dofs]), pieces)
    stars = by_partition(star, pieces)
    local_flux = by_partition(flux_local, pieces)
    neigh_flux = by_partition(flux_neighbor, pieces)
    clusters = by_partition(cluster, pieces)
    kinds = by_partition(face_kind, pieces)
    indices = by_partition(neighbor_index, pieces)
    others = by_partition(neighbor_face, pieces)
    rotation = by_partition(orientation, pieces)
    senders = by_partition(send_element, pieces)
    sender_faces = by_partition(send_face, pieces)
    offset_table = jnp.array(OFFSETS, jnp.int32)
    part_ids = jnp.arange(pieces, dtype=jnp.int32)
    step_size = 0.5 * jnp.min(timescale)
    fine_mask = clusters == 0

    def integrate(fields_now, start_time, end_time):
        def single(packed):
            blocks, matrices, begin_time, finish = packed
            return integral(expansion(blocks, matrices, stiffness), begin_time, finish)
        return lax.map(single, (fields_now, stars, start_time, end_time))

    def updates(integrals):
        def rows_of(blocks):
            faced = jnp.einsum('fba,naqe->fenbq', face_proj, blocks, precision=highest)
            return faced.reshape(4 * ELEMENTS, 2 * FACE_BASIS * QUANT)
        lookup = lax.map(rows_of, integrals).reshape(pieces * 4 * ELEMENTS, 2 * FACE_BASIS * QUANT)

        def single(packed):
            part_id, blocks, matrices, loc_part, nbr_part, kind_part, index_part, other_part, turn_part = packed
            base_row = part_id * 4 * ELEMENTS
            own_rows = base_row + jnp.arange(4, dtype=jnp.int32)[:, None] * ELEMENTS + jnp.arange(ELEMENTS, dtype=jnp.int32)[None, :]
            local_rows = base_row + other_part * ELEMENTS + index_part
            group_index = index_part // SLOTS
            position = index_part % SLOTS
            source = jnp.clip(part_id + offset_table[group_index], 0, pieces - 1)
            sender = senders[source, group_index, position]
            sender_side = sender_faces[source, group_index, position]
            remote_rows = source * 4 * ELEMENTS + sender_side * ELEMENTS + sender
            row_index = jnp.where(kind_part == 1, remote_rows, jnp.where(kind_part == 0, local_rows, own_rows)).astype(jnp.int32)
            gathered = jnp.take(lookup, row_index.reshape(-1), axis=0).reshape(4, ELEMENTS, 2, FACE_BASIS, QUANT)
            gathered = jnp.transpose(gathered, (2, 3, 4, 0, 1))
            own_faces = face_values(blocks, face_proj)
            return face_update(blocks, own_faces, gathered, kind_part, turn_part, loc_part, nbr_part, face_orient, face_lift, stiffness, matrices)
        return lax.map(single, (part_ids, integrals, stars, local_flux, neigh_flux, kinds, indices, others, rotation))

    zero_time = jnp.zeros((pieces, ELEMENTS), jnp.float32)
    opening = integrate(fields, zero_time, zero_time + step_size)
    update_first = updates(opening)
    fine_full = fine_mask[:, None, None, None, :]
    fields_one = jnp.where(fine_full, fields + update_first, fields)
    closing = integrate(fields_one, jnp.where(fine_mask, 0.0, step_size), jnp.where(fine_mask, step_size, 2.0 * step_size))
    update_second = updates(closing)
    middle = (clusters == 1)[:, None, None, None, :]
    result_fields = jnp.where(fine_full, fields_one + update_second, jnp.where(middle, fields + update_first + update_second, fields))
    sensitivity = jnp.sum(opening[:, 0] * opening[:, 1], axis=(1, 2)) + jnp.sum(closing[:, 0] * closing[:, 1], axis=(1, 2))
    return from_partition(result_fields[:, 0]), from_partition(result_fields[:, 1]), from_partition(sensitivity)
```

```python
import math

import jax
import jax.numpy as jnp
from jax import lax
from jax.experimental import pallas as pl
from jax.experimental.pallas import tpu as pltpu
from jax.sharding import PartitionSpec as P

BASIS = 35
FACE_BASIS = 15
QUANT = 9
ORDER = 5
ROWS = 40
PACK = 48
FROWS = 16
ELEMS = 256
SLOTS = 64
HALF = 128
TABLE = QUANT * FROWS
MIRRORED = (0, 3, 5)
F32 = jnp.float32
BF16 = jnp.bfloat16
VMEM_LIMIT = 16 * 1024 * 1024


def dot(a, b):
    return jnp.dot(a, b, preferred_element_type=F32)


def split(x):
    hi = x.astype(BF16)
    return hi, (x - hi.astype(F32)).astype(BF16)


def place(mat, cols, hi_at, lo_at):
    rows = mat.shape[1]
    gap = lax.broadcasted_iota(jnp.int32, (rows, cols), 1) - lax.broadcasted_iota(
        jnp.int32, (rows, cols), 0
    )

    def ones(starts):
        mask = gap == starts[0]
        for start in starts[1:]:
            mask = mask | (gap == start)
        return jnp.where(mask, 1.0, 0.0).astype(BF16)

    hi, lo = split(mat)
    return dot(hi, ones(hi_at)) + dot(lo, ones(lo_at))


def fill_stiff(out, stage, stiffness, transposed):
    stage[...] = jnp.zeros(stage.shape, F32)
    for d in range(3):
        mat = stiffness[d]
        if transposed:
            mat = mat.T
        stage[d * ROWS : d * ROWS + BASIS, 0 : 3 * PACK] = place(
            mat, 3 * PACK, (0, PACK), (2 * PACK,)
        )
    out[...] = stage[0 : 3 * ROWS, 0 : 3 * PACK].astype(BF16)


def fill_proj(out, stage, face_proj):
    stage[...] = jnp.zeros(stage.shape, F32)
    for f in range(4):
        stage[f * FROWS : f * FROWS + FACE_BASIS, 0 : 3 * PACK] = place(
            face_proj[:, f, :], 3 * PACK, (0, PACK), (2 * PACK,)
        )
    out[...] = stage[0 : 4 * FROWS, 0 : 3 * PACK].astype(BF16)


def fill_orient(out, stage, face_orient):
    stage[...] = jnp.zeros(stage.shape, F32)
    for o in range(3):
        stage[o * FROWS : o * FROWS + FACE_BASIS, 0 : 3 * FROWS] = place(
            face_orient[o], 3 * FROWS, (0, FROWS), (2 * FROWS,)
        )
    out[...] = stage[0 : 3 * FROWS, 0 : 3 * FROWS].astype(BF16)


def fill_lift(out, stage, face_lift):
    stage[...] = jnp.zeros(stage.shape, F32)
    total = jnp.zeros((BASIS, 12 * FROWS), F32)
    for f in range(4):
        base = f * FROWS
        total = total + place(
            face_lift[:, f, :].T, 12 * FROWS, (base, 4 * FROWS + base), (8 * FROWS + base,)
        )
    stage[0:BASIS, 0 : 12 * FROWS] = total
    out[...] = stage[0:ROWS, 0 : 12 * FROWS].astype(BF16)


def stack_split(x3, q, x):
    hi, lo = split(jnp.concatenate([x, jnp.zeros((PACK - ROWS, x.shape[1]), F32)], 0))
    x3[q, 0:PACK, :] = hi
    x3[q, PACK : 2 * PACK, :] = lo
    x3[q, 2 * PACK : 3 * PACK, :] = hi


def star_apply(spread, star, adjoint, half, emit):
    lanes = slice(half * HALF, half * HALF + HALF)
    acc = [None] * QUANT
    for p in range(QUANT):
        for d in range(3):
            value = spread[p, d * ROWS : d * ROWS + ROWS, lanes]
            for q in range(QUANT):
                if adjoint:
                    weight = star[p, q, d : d + 1, lanes]
                else:
                    weight = star[q, p, d : d + 1, lanes]
                term = value * weight
                acc[q] = term if acc[q] is None else acc[q] + term
    for q in range(QUANT):
        emit(q, lanes, acc[q])


def project(x3, wproj, table, n, faces=None):
    for q in range(QUANT):
        value = dot(wproj[...], x3[q])
        if faces is not None:
            faces[n, q] = value
        hi, lo = split(value)
        for f in range(4):
            lanes = slice(f * ELEMS, f * ELEMS + ELEMS)
            rows = slice(f * FROWS, f * FROWS + FROWS)
            base = n * 2 * TABLE + q * FROWS
            table[base : base + FROWS, lanes] = hi[rows]
            table[base + TABLE : base + TABLE + FROWS, lanes] = lo[rows]


def pack_send(table, pick, emit):
    found = dot(table[...], pick[...])
    low = lax.broadcasted_iota(jnp.int32, (TABLE, HALF), 1) < SLOTS
    sides = [
        found[n * 2 * TABLE : n * 2 * TABLE + TABLE]
        + found[n * 2 * TABLE + TABLE : n * 2 * TABLE + 2 * TABLE]
        for n in range(2)
    ]
    for pair in range(2):
        lanes = slice(pair * HALF, pair * HALF + HALF)
        first = sides[0][:, lanes]
        second = sides[1][:, lanes]
        emit(2 * pair, jnp.where(low, first, pltpu.roll(second, SLOTS, 1)))
        emit(2 * pair + 1, jnp.where(low, pltpu.roll(first, SLOTS, 1), second))


def unpack_received(groups, table):
    low = lax.broadcasted_iota(jnp.int32, (TABLE, HALF), 1) < SLOTS
    for pair in range(2):
        lanes = slice(pair * HALF, pair * HALF + HALF)
        first = groups[2 * pair]
        second = groups[2 * pair + 1]
        for n, value in enumerate(
            (
                jnp.where(low, first, pltpu.roll(second, SLOTS, 1)),
                jnp.where(low, pltpu.roll(first, SLOTS, 1), second),
            )
        ):
            hi, lo = split(value)
            table[n * 2 * TABLE : n * 2 * TABLE + TABLE, lanes] = hi
            table[n * 2 * TABLE + TABLE : n * 2 * TABLE + 2 * TABLE, lanes] = lo


def one_hot(codes, first, rows):
    ids = lax.broadcasted_iota(jnp.int32, (rows, codes.shape[1]), 0) + first
    return jnp.where(ids == codes, 1.0, 0.0).astype(BF16)


def first_kernel(
    fwd,
    adj,
    star,
    stiffness,
    face_proj,
    send_element,
    send_face,
    face_kind,
    neighbor_index,
    neighbor_face,
    cluster,
    orientation,
    face_lift,
    face_orient,
    flux_local,
    flux_neighbor,
    derived,
    pick_local,
    pick_remote,
    pick_send,
    pick_fine,
    fine_star,
    wstiff,
    wstiff_t,
    wproj,
    wlift,
    worient,
    star_kept,
    local_kept,
    neighbor_kept,
    kind_kept,
    turn_kept,
    cluster_kept,
    stage,
    x3,
    spread,
    codes,
    series,
    sems,
):
    copies = [
        pltpu.make_async_copy(source, kept, sems.at[ORDER - 1 + i])
        for i, (source, kept) in enumerate(
            ((star, star_kept), (flux_local, local_kept), (flux_neighbor, neighbor_kept))
        )
    ]
    for copy in copies:
        copy.start()
    star = star_kept
    kind_kept[...] = face_kind[...]
    turn_kept[...] = orientation[...]
    cluster_kept[...] = cluster[...]
    fill_stiff(wstiff, stage, stiffness, False)
    fill_stiff(wstiff_t, stage, stiffness, True)
    fill_proj(wproj, stage, face_proj)
    fill_lift(wlift, stage, face_lift)
    fill_orient(worient, stage, face_orient)

    for n, field in enumerate((fwd, adj)):
        for q in range(QUANT):
            series[0, n, q, 0:BASIS, :] = field[q]
            series[0, n, q, BASIS:ROWS, :] = jnp.zeros((ROWS - BASIS, ELEMS), F32)

    send_code = send_face[...] * ELEMS + send_element[...]
    for g in range(4):
        codes[0:1, g * SLOTS : g * SLOTS + SLOTS] = send_code[g : g + 1]
    for block in range(4):
        rows = slice(block * ELEMS, block * ELEMS + ELEMS)
        pick_send[rows, :] = one_hot(codes[0:1, :], block * ELEMS, ELEMS)
    for f in range(4):
        lanes = slice(f * ELEMS, f * ELEMS + ELEMS)
        kind = face_kind[f : f + 1, :]
        index = neighbor_index[f : f + 1, :]
        local = jnp.where(kind == 0, neighbor_face[f : f + 1, :] * ELEMS + index, -1)
        remote = jnp.where(kind == 1, index, -1)
        for block in range(4):
            rows = slice(block * ELEMS, block * ELEMS + ELEMS)
            pick_local[rows, lanes] = one_hot(local, block * ELEMS, ELEMS)
        pick_remote[:, lanes] = one_hot(remote, 0, ELEMS)

    fine = cluster[...] == 0
    upper = lax.broadcasted_iota(jnp.int32, (ELEMS, ELEMS), 0) < lax.broadcasted_iota(
        jnp.int32, (ELEMS, ELEMS), 1
    )
    flags = jnp.broadcast_to(jnp.where(fine, 1.0, 0.0), (FROWS, ELEMS)).astype(BF16)
    rank = dot(flags, jnp.where(upper, 1.0, 0.0).astype(BF16))[0:1]
    place_of = jnp.where(fine, rank.astype(jnp.int32), -1)
    slot = lax.broadcasted_iota(jnp.int32, (HALF, ELEMS), 0)
    slot = jnp.where(slot < SLOTS, slot, slot - SLOTS)
    chosen = jnp.where(slot == place_of, 1.0, 0.0)
    pick_fine[...] = chosen.astype(BF16)
    pick_t = chosen.T.astype(BF16)
    low1 = lax.broadcasted_iota(jnp.int32, (1, HALF), 1) < SLOTS
    copies[0].wait()
    for d in range(3):
        plain = []
        for q in range(QUANT):
            hi, lo = split(star[q, :, d, :])
            plain.append(dot(hi, pick_t) + dot(lo, pick_t))
        for q in range(QUANT):
            for p in range(QUANT):
                fine_star[q, p, d : d + 1, :] = jnp.where(
                    low1, plain[q][p : p + 1], plain[p][q : q + 1]
                )

    def step(degree, _):
        for n in range(2):
            for q in range(QUANT):
                stack_split(x3, q, series[degree, n, q])
            for q in range(QUANT):
                spread[q] = dot(wstiff[...], x3[q])
            for half in range(2):

                def emit(q, lanes, value):
                    series[degree + 1, n, q, :, lanes] = value

                star_apply(spread, star, n == 1, half, emit)
        pltpu.make_async_copy(series.at[degree + 1], derived.at[degree], sems.at[degree]).start()
        return 0

    lax.fori_loop(0, ORDER - 1, step, 0)
    copies[1].wait()
    copies[2].wait()
    for degree in range(ORDER - 1):
        pltpu.make_async_copy(series.at[degree + 1], derived.at[degree], sems.at[degree]).wait()


def weights_of(steps):
    dt = 0.5 * jnp.min(steps[...])
    early = []
    late = []
    power = dt
    for degree in range(ORDER):
        scale = 1.0 / math.factorial(degree + 1)
        early.append(power * scale)
        late.append(power * (scale * (2.0 ** (degree + 1) - 1.0)))
        power = power * dt
    return early, late


def integral_kernel(
    steps,
    fwd,
    adj,
    derived,
    pick_send,
    wproj,
    out0,
    out1,
    out2,
    out3,
    integral,
    later,
    faces,
    table,
    x3,
    series,
    sems,
):
    outs = (out0, out1, out2, out3)
    copies = [
        pltpu.make_async_copy(derived.at[degree], series.at[degree], sems.at[degree])
        for degree in range(ORDER - 1)
    ]
    for copy in copies:
        copy.start()
    early, late = weights_of(steps)
    for n, field in enumerate((fwd, adj)):
        for q in range(QUANT):
            for sums, weight in ((integral, early[0]), (later, late[0])):
                sums[n, q, 0:BASIS, :] = weight * field[q]
                sums[n, q, BASIS:ROWS, :] = jnp.zeros((ROWS - BASIS, ELEMS), F32)
    for copy in copies:
        copy.wait()
    for n in range(2):
        for q in range(QUANT):
            total = integral[n, q]
            after = later[n, q]
            for degree in range(1, ORDER):
                value = series[degree - 1, n, q]
                total = total + early[degree] * value
                after = after + late[degree] * value
            integral[n, q] = total
            later[n, q] = after
            stack_split(x3.at[n], q, total)
        project(x3.at[n], wproj, table, n, faces)

    def send(g, value):
        outs[g][...] = value

    pack_send(table, pick_send, send)


def flux_apply(source, weights, adjoint, n, f, half, acc):
    lanes = slice(half * HALF, half * HALF + HALF)
    rows = slice(f * FROWS, f * FROWS + FROWS)
    for p in range(QUANT):
        value = source[n, p, rows, lanes]
        for q in range(QUANT):
            if adjoint:
                weight = weights[p, q, f : f + 1, lanes]
            else:
                weight = weights[q, p, f : f + 1, lanes]
            term = value * weight
            acc[q] = term if acc[q] is None else acc[q] + term
    return acc


def local_part(
    x3, wstiff_t, spread, star, faces, table, flux_local, pick_local, volume, flux_sum, gathered
):
    for n in range(2):
        for q in range(QUANT):
            spread[q] = dot(wstiff_t[...], x3[n, q])
        for half in range(2):

            def emit(q, lanes, value):
                volume[n, q, :, lanes] = value

            star_apply(spread, star, n == 1, half, emit)
    for f in range(4):
        lanes = slice(f * ELEMS, f * ELEMS + ELEMS)
        found = dot(table[...], pick_local[:, lanes])
        for n in range(2):
            gathered[n, f] = (
                found[n * 2 * TABLE : n * 2 * TABLE + TABLE]
                + found[n * 2 * TABLE + TABLE : n * 2 * TABLE + 2 * TABLE]
            )
    for n in range(2):
        for f in range(4):
            for half in range(2):
                acc = flux_apply(faces, flux_local, n == 1, n, f, half, [None] * QUANT)
                for q in range(QUANT):
                    flux_sum[
                        n,
                        q,
                        f * FROWS : f * FROWS + FROWS,
                        half * HALF : half * HALF + HALF,
                    ] = acc[q]


def remote_part(
    groups,
    rtable,
    pick_remote,
    gathered,
    faces,
    face_kind,
    orientation,
    worient,
    x3o,
    other,
    flux_sum,
    flux_neighbor,
    x3l,
    wlift,
    volume,
    emit,
):
    unpack_received(groups, rtable)
    for f in range(4):
        lanes = slice(f * ELEMS, f * ELEMS + ELEMS)
        rows = slice(f * FROWS, f * FROWS + FROWS)
        found = dot(rtable[...], pick_remote[:, lanes])
        turn = orientation[f : f + 1, :]
        surface = face_kind[f : f + 1, :] == 2
        for n in range(2):
            total = (
                found[n * 2 * TABLE : n * 2 * TABLE + TABLE]
                + found[n * 2 * TABLE + TABLE : n * 2 * TABLE + 2 * TABLE]
                + gathered[n, f]
            )
            hi, lo = split(total)
            for q in range(QUANT):
                part = slice(q * FROWS, q * FROWS + FROWS)
                x3o[n, f, q, 0:FROWS, :] = hi[part]
                x3o[n, f, q, FROWS : 2 * FROWS, :] = lo[part]
                x3o[n, f, q, 2 * FROWS : 3 * FROWS, :] = hi[part]
            for q in range(QUANT):
                three = dot(worient[...], x3o[n, f, q])
                turned = jnp.where(
                    turn == 0,
                    three[0:FROWS],
                    jnp.where(turn == 1, three[FROWS : 2 * FROWS], three[2 * FROWS : 3 * FROWS]),
                )
                own = faces[n, q, rows, :]
                if q in MIRRORED:
                    own = -own
                other[n, q, rows, :] = turned + jnp.where(surface, own, 0.0)
    for n in range(2):
        for f in range(4):
            rows = slice(f * FROWS, f * FROWS + FROWS)
            for half in range(2):
                lanes = slice(half * HALF, half * HALF + HALF)
                acc = [flux_sum[n, q, rows, lanes] for q in range(QUANT)]
                acc = flux_apply(other, flux_neighbor, n == 1, n, f, half, acc)
                for q in range(QUANT):
                    hi, lo = split(acc[q])
                    x3l[q, f * FROWS : f * FROWS + FROWS, lanes] = hi
                    x3l[q, (4 + f) * FROWS : (5 + f) * FROWS, lanes] = lo
                    x3l[q, (8 + f) * FROWS : (9 + f) * FROWS, lanes] = hi
        for q in range(QUANT):
            emit(n, q, volume[n, q] + dot(wlift[...], x3l[q]))


def middle_kernel(
    steps,
    fwd,
    adj,
    integral,
    later,
    in0,
    in1,
    in2,
    in3,
    pick_remote,
    pick_send,
    pick_fine,
    fine_star,
    gathered,
    faces,
    face_kind,
    orientation,
    worient,
    flux_sum,
    flux_neighbor,
    wlift,
    volume,
    cluster,
    wstiff,
    wproj,
    out0,
    out1,
    out2,
    out3,
    base,
    faces_out,
    table,
    x3,
    sens,
    rtable,
    x3o,
    other,
    x3l,
    wide,
    x3c,
    spread_c,
    fields_c,
):
    outs = (out0, out1, out2, out3)
    early, _ = weights_of(steps)
    fine = cluster[...] == 0
    active = cluster[...] <= 1

    def emit_first(n, q, value):
        start = jnp.concatenate([(fwd, adj)[n][q], jnp.zeros((ROWS - BASIS, ELEMS), F32)], 0)
        moved = start + value
        base[n, q] = jnp.where(active, moved, start)
        hi, lo = split(moved)
        wide[q, 0:ROWS, 2 * n * ELEMS : (2 * n + 1) * ELEMS] = hi
        wide[q, 0:ROWS, (2 * n + 1) * ELEMS : (2 * n + 2) * ELEMS] = lo

    wide[...] = jnp.zeros(wide.shape, BF16)
    remote_part(
        [in0[...], in1[...], in2[...], in3[...]],
        rtable,
        pick_remote,
        gathered,
        faces,
        face_kind,
        orientation,
        worient,
        x3o,
        other,
        flux_sum,
        flux_neighbor,
        x3l,
        wlift,
        volume,
        emit_first,
    )

    slot = lax.broadcasted_iota(jnp.int32, (HALF, ELEMS), 0)
    chosen = pick_fine[...].astype(F32)
    mine = [jnp.where(slot < SLOTS, chosen, 0.0), jnp.where(slot < SLOTS, 0.0, chosen)]
    pick_t = [m.T.astype(BF16) for m in mine]
    mine = [m.astype(BF16) for m in mine]
    for q in range(QUANT):
        value = jnp.zeros((ROWS, HALF), F32)
        for n in range(2):
            for part in range(2):
                lanes = slice((2 * n + part) * ELEMS, (2 * n + part + 1) * ELEMS)
                value = value + dot(wide[q, :, lanes], pick_t[n])[0:ROWS]
        fields_c[q] = early[0] * value
        stack_split(x3c, q, value)
    for degree in range(1, ORDER):
        for q in range(QUANT):
            spread_c[q] = dot(wstiff[...], x3c[q])

        def emit(q, lanes, value):
            fields_c[q] = fields_c[q] + early[degree] * value
            if degree < ORDER - 1:
                stack_split(x3c, q, value)

        star_apply(spread_c, fine_star, False, 0, emit)

    products = jnp.zeros((ROWS, ELEMS), F32)
    for q in range(QUANT):
        hi, lo = split(jnp.concatenate([fields_c[q], jnp.zeros((PACK - ROWS, HALF), F32)], 0))
        both = []
        for n in range(2):
            renewed = (dot(hi, mine[n]) + dot(lo, mine[n]))[0:ROWS]
            value = jnp.where(fine, renewed, later[n, q])
            stack_split(x3.at[n], q, value)
            both.append(value)
        products = products + integral[0, q] * integral[1, q] + both[0] * both[1]
    sens[...] = jnp.sum(products, axis=0, keepdims=True)
    for n in range(2):
        project(x3.at[n], wproj, table, n, faces_out)

    def send(g, value):
        outs[g][...] = value

    pack_send(table, pick_send, send)


def local_kernel(
    x3, star, faces, table, flux_local, pick_local, wstiff_t, volume, flux_sum, gathered, spread
):
    local_part(
        x3, wstiff_t, spread, star, faces, table, flux_local, pick_local, volume, flux_sum, gathered
    )


def last_kernel(
    in0,
    in1,
    in2,
    in3,
    pick_remote,
    gathered,
    faces,
    face_kind,
    orientation,
    worient,
    flux_sum,
    flux_neighbor,
    wlift,
    volume,
    base,
    cluster,
    fwd,
    adj,
    rtable,
    x3o,
    other,
    x3l,
):
    active = cluster[...] <= 1
    outs = (fwd, adj)

    def emit(n, q, value):
        final = base[n, q] + jnp.where(active, value, 0.0)
        outs[n][q] = final[0:BASIS]

    remote_part(
        [in0[...], in1[...], in2[...], in3[...]],
        rtable,
        pick_remote,
        gathered,
        faces,
        face_kind,
        orientation,
        worient,
        x3o,
        other,
        flux_sum,
        flux_neighbor,
        x3l,
        wlift,
        volume,
        emit,
    )


def call(kernel, args, outs, scratch, flops, spaces=None, out_spaces=None, far=()):
    whole = pl.BlockSpec(memory_space=pltpu.VMEM)
    spaces = spaces or {}
    out_spaces = out_spaces or {}
    args = [
        pltpu.with_memory_space_constraint(x, pltpu.HBM if i in far else pltpu.VMEM)
        for i, x in enumerate(args)
    ]
    return pl.pallas_call(
        kernel,
        out_shape=outs,
        in_specs=[spaces.get(i, whole) for i in range(len(args))],
        out_specs=tuple(out_spaces.get(i, whole) for i in range(len(outs))),
        scratch_shapes=scratch,
        compiler_params=pltpu.CompilerParams(vmem_limit_bytes=VMEM_LIMIT),
        cost_estimate=pl.CostEstimate(flops=flops, bytes_accessed=4000000, transcendentals=0),
    )(*args)


def keep(*shape, dtype=F32):
    return pltpu.VMEM(shape, dtype)


def deliver(outgoing):
    received = []
    for value, by in zip(outgoing, (2, 1, -1, -2)):
        length = lax.axis_size("dom")
        pairs = [(i, (i + by) % length) for i in range(length)]
        received.append(lax.ppermute(value, "dom", pairs))
    return received


def shards(
    fwd_dofs,
    adj_dofs,
    star,
    flux_local,
    flux_neighbor,
    timescale,
    cluster,
    face_kind,
    neighbor_index,
    neighbor_face,
    orientation,
    send_element,
    send_face,
    stiffness,
    face_proj,
    face_lift,
    face_orient,
):
    count = lax.axis_size("dom")
    halves = jnp.minimum(timescale[:HALF], timescale[HALF:])
    steps = lax.all_to_all(jnp.broadcast_to(halves[None], (count, HALF)), "dom", 0, 0)
    cluster = cluster.reshape(1, ELEMS)

    fwd_dofs = jnp.transpose(fwd_dofs, (1, 0, 2))
    adj_dofs = jnp.transpose(adj_dofs, (1, 0, 2))
    star = jnp.transpose(star, (1, 2, 0, 3))
    flux_local = jnp.transpose(flux_local, (1, 2, 0, 3))
    flux_neighbor = jnp.transpose(flux_neighbor, (1, 2, 0, 3))
    face_proj = jnp.transpose(face_proj, (1, 0, 2))
    face_lift = jnp.transpose(face_lift, (2, 0, 1))

    bf16 = {"dtype": BF16}
    whole = pl.BlockSpec(memory_space=pltpu.VMEM)
    away = pl.BlockSpec(memory_space=pl.ANY)
    message = keep(TABLE, HALF)
    face_data = keep(2, QUANT, 4 * FROWS, ELEMS)
    table_data = keep(4 * TABLE, 4 * ELEMS, **bf16)
    stacked = keep(2, QUANT, 3 * PACK, ELEMS, **bf16)
    fields = keep(2, QUANT, ROWS, ELEMS)
    apart = (ORDER - 1, 2, QUANT, ROWS, ELEMS)
    spread = keep(QUANT, 3 * ROWS, ELEMS)
    remote_scratch = (
        keep(4 * TABLE, ELEMS, **bf16),
        keep(2, 4, QUANT, 3 * FROWS, ELEMS, **bf16),
        face_data,
        keep(QUANT, 12 * FROWS, ELEMS, **bf16),
    )

    (
        derived,
        pick_local,
        pick_remote,
        pick_send,
        pick_fine,
        fine_star,
        wstiff,
        wstiff_t,
        wproj,
        wlift,
        worient,
        star,
        flux_local,
        flux_neighbor,
        face_kind,
        orientation,
        cluster,
    ) = call(
        first_kernel,
        (
            fwd_dofs,
            adj_dofs,
            star,
            stiffness,
            face_proj,
            send_element,
            send_face,
            face_kind,
            neighbor_index,
            neighbor_face,
            cluster,
            orientation,
            face_lift,
            face_orient,
            flux_local,
            flux_neighbor,
        ),
        (
            pltpu.HBM(apart, F32),
            pltpu.HBM((4 * ELEMS, 4 * ELEMS), BF16),
            keep(ELEMS, 4 * ELEMS, **bf16),
            keep(4 * ELEMS, ELEMS, **bf16),
            keep(HALF, ELEMS, **bf16),
            keep(QUANT, QUANT, 3, HALF),
            keep(3 * ROWS, 3 * PACK, **bf16),
            keep(3 * ROWS, 3 * PACK, **bf16),
            keep(4 * FROWS, 3 * PACK, **bf16),
            keep(ROWS, 12 * FROWS, **bf16),
            keep(3 * FROWS, 3 * FROWS, **bf16),
            keep(*star.shape),
            keep(*flux_local.shape),
            keep(*flux_neighbor.shape),
            keep(4, ELEMS, dtype=jnp.int32),
            keep(4, ELEMS, dtype=jnp.int32),
            keep(1, ELEMS, dtype=jnp.int32),
        ),
        (
            keep(128, 256),
            keep(QUANT, 3 * PACK, ELEMS, **bf16),
            spread,
            keep(8, ELEMS, dtype=jnp.int32),
            keep(ORDER, 2, QUANT, ROWS, ELEMS),
            pltpu.SemaphoreType.DMA((ORDER + 2,)),
        ),
        14000000000,
        far=range(16),
        spaces={2: away, 14: away, 15: away},
        out_spaces={0: away},
    )

    def local(x3, faces, table):
        return call(
            local_kernel,
            (x3, star, faces, table, flux_local, pick_local, wstiff_t),
            (keep(2, QUANT, ROWS, ELEMS), face_data, keep(2, 4, TABLE, ELEMS)),
            (spread,),
            4000000000,
        )

    *outgoing, integral, later, faces, table, x3 = call(
        integral_kernel,
        (steps, fwd_dofs, adj_dofs, derived, pick_send, wproj),
        (message,) * 4 + (fields, fields, face_data, table_data, stacked),
        (keep(*apart), pltpu.SemaphoreType.DMA((ORDER - 1,))),
        2000000000,
        spaces={3: away},
        far=(1, 2, 3),
    )
    received = deliver(outgoing)
    volume, flux_sum, gathered = local(x3, faces, table)

    *outgoing, base, faces, table, x3, sens = call(
        middle_kernel,
        (
            steps,
            fwd_dofs,
            adj_dofs,
            integral,
            later,
            *received,
            pick_remote,
            pick_send,
            pick_fine,
            fine_star,
            gathered,
            faces,
            face_kind,
            orientation,
            worient,
            flux_sum,
            flux_neighbor,
            wlift,
            volume,
            cluster,
            wstiff,
            wproj,
        ),
        (message,) * 4
        + (keep(2, QUANT, ROWS, ELEMS), face_data, table_data, stacked, keep(1, ELEMS)),
        remote_scratch
        + (
            keep(QUANT, PACK, 4 * ELEMS, **bf16),
            keep(QUANT, 3 * PACK, HALF, **bf16),
            keep(QUANT, 3 * ROWS, HALF),
            keep(QUANT, ROWS, HALF),
        ),
        8000000000,
    )
    received = deliver(outgoing)
    volume, flux_sum, gathered = local(x3, faces, table)

    fwd_final, adj_final = call(
        last_kernel,
        (
            *received,
            pick_remote,
            gathered,
            faces,
            face_kind,
            orientation,
            worient,
            flux_sum,
            flux_neighbor,
            wlift,
            volume,
            base,
            cluster,
        ),
        (
            jax.ShapeDtypeStruct(fwd_dofs.shape, F32),
            jax.ShapeDtypeStruct(adj_dofs.shape, F32),
        ),
        remote_scratch,
        4000000000,
    )
    return (
        jnp.transpose(fwd_final, (1, 0, 2)),
        jnp.transpose(adj_final, (1, 0, 2)),
        sens.reshape(ELEMS),
    )


def solution(mesh):
    return jax.shard_map(
        shards,
        mesh=mesh,
        in_specs=(
            P(None, None, "dom"),
            P(None, None, "dom"),
            P(None, None, None, "dom"),
            P(None, None, None, "dom"),
            P(None, None, None, "dom"),
            P("dom"),
            P("dom"),
            P(None, "dom"),
            P(None, "dom"),
            P(None, "dom"),
            P(None, "dom"),
            P(None, "dom"),
            P(None, "dom"),
            P(),
            P(),
            P(),
            P(),
        ),
        out_specs=(P(None, None, "dom"), P(None, None, "dom"), P("dom")),
        check_vma=False,
    )
```

```python
import math

import jax
import jax.numpy as jnp
from jax import lax
from jax.experimental import pallas as pl
from jax.experimental.pallas import tpu as pltpu
from jax.sharding import PartitionSpec as P

BASIS = 35
FACE_BASIS = 15
QUANT = 9
ORDER = 5
ROWS = 40
PACK = 48
FROWS = 16
ELEMS = 256
SLOTS = 64
HALF = 128
TABLE = QUANT * FROWS
MIRRORED = (0, 3, 5)
F32 = jnp.float32
BF16 = jnp.bfloat16
VMEM_LIMIT = 16 * 1024 * 1024


def dot(a, b):
    return jnp.dot(a, b, preferred_element_type=F32)


def split(x):
    hi = x.astype(BF16)
    return hi, (x - hi.astype(F32)).astype(BF16)


def place(mat, cols, hi_at, lo_at):
    rows = mat.shape[1]
    gap = lax.broadcasted_iota(jnp.int32, (rows, cols), 1) - lax.broadcasted_iota(
        jnp.int32, (rows, cols), 0
    )

    def ones(starts):
        mask = gap == starts[0]
        for start in starts[1:]:
            mask = mask | (gap == start)
        return jnp.where(mask, 1.0, 0.0).astype(BF16)

    hi, lo = split(mat)
    return dot(hi, ones(hi_at)) + dot(lo, ones(lo_at))


def fill_stiff(out, stage, stiffness, transposed):
    stage[...] = jnp.zeros(stage.shape, F32)
    for d in range(3):
        mat = stiffness[d]
        if transposed:
            mat = mat.T
        stage[d * ROWS : d * ROWS + BASIS, 0 : 3 * PACK] = place(
            mat, 3 * PACK, (0, PACK), (2 * PACK,)
        )
    out[...] = stage[0 : 3 * ROWS, 0 : 3 * PACK].astype(BF16)


def fill_proj(out, stage, face_proj):
    stage[...] = jnp.zeros(stage.shape, F32)
    for f in range(4):
        stage[f * FROWS : f * FROWS + FACE_BASIS, 0 : 3 * PACK] = place(
            face_proj[:, f, :], 3 * PACK, (0, PACK), (2 * PACK,)
        )
    out[...] = stage[0 : 4 * FROWS, 0 : 3 * PACK].astype(BF16)


def fill_orient(out, stage, face_orient):
    stage[...] = jnp.zeros(stage.shape, F32)
    for o in range(3):
        stage[o * FROWS : o * FROWS + FACE_BASIS, 0 : 3 * FROWS] = place(
            face_orient[o], 3 * FROWS, (0, FROWS), (2 * FROWS,)
        )
    out[...] = stage[0 : 3 * FROWS, 0 : 3 * FROWS].astype(BF16)


def fill_lift(out, stage, face_lift):
    stage[...] = jnp.zeros(stage.shape, F32)
    total = jnp.zeros((BASIS, 12 * FROWS), F32)
    for f in range(4):
        base = f * FROWS
        total = total + place(
            face_lift[:, f, :].T, 12 * FROWS, (base, 4 * FROWS + base), (8 * FROWS + base,)
        )
    stage[0:BASIS, 0 : 12 * FROWS] = total
    out[...] = stage[0:ROWS, 0 : 12 * FROWS].astype(BF16)


def stack_split(x3, q, x):
    hi, lo = split(jnp.concatenate([x, jnp.zeros((PACK - ROWS, x.shape[1]), F32)], 0))
    x3[q, 0:PACK, :] = hi
    x3[q, PACK : 2 * PACK, :] = lo
    x3[q, 2 * PACK : 3 * PACK, :] = hi


def stack_pair(x3, q, x):
    hi, lo = split(jnp.concatenate([x, jnp.zeros((PACK - ROWS, HALF), F32)], 0))
    lanes = slice(q % 2 * HALF, q % 2 * HALF + HALF)
    x3[q // 2, 0:PACK, lanes] = hi
    x3[q // 2, PACK : 2 * PACK, lanes] = lo
    x3[q // 2, 2 * PACK : 3 * PACK, lanes] = hi


def star_apply(spread, star, adjoint, half, emit):
    lanes = slice(half * HALF, half * HALF + HALF)
    acc = [None] * QUANT
    for p in range(QUANT):
        for d in range(3):
            value = spread[p, d * ROWS : d * ROWS + ROWS, lanes]
            for q in range(QUANT):
                if adjoint:
                    weight = star[p, q, d : d + 1, lanes]
                else:
                    weight = star[q, p, d : d + 1, lanes]
                term = value * weight
                acc[q] = term if acc[q] is None else acc[q] + term
    for q in range(QUANT):
        emit(q, lanes, acc[q])


def project(x3, wproj, table, n, faces=None):
    for q in range(QUANT):
        value = dot(wproj[...], x3[q])
        if faces is not None:
            faces[n, q] = value
        hi, lo = split(value)
        for f in range(4):
            lanes = slice(f * ELEMS, f * ELEMS + ELEMS)
            rows = slice(f * FROWS, f * FROWS + FROWS)
            base = n * 2 * TABLE + q * FROWS
            table[base : base + FROWS, lanes] = hi[rows]
            table[base + TABLE : base + TABLE + FROWS, lanes] = lo[rows]


def pack_send(table, pick, emit):
    found = dot(table[...], pick[...])
    low = lax.broadcasted_iota(jnp.int32, (TABLE, HALF), 1) < SLOTS
    sides = [
        found[n * 2 * TABLE : n * 2 * TABLE + TABLE]
        + found[n * 2 * TABLE + TABLE : n * 2 * TABLE + 2 * TABLE]
        for n in range(2)
    ]
    for pair in range(2):
        lanes = slice(pair * HALF, pair * HALF + HALF)
        first = sides[0][:, lanes]
        second = sides[1][:, lanes]
        emit(2 * pair, jnp.where(low, first, pltpu.roll(second, SLOTS, 1)))
        emit(2 * pair + 1, jnp.where(low, pltpu.roll(first, SLOTS, 1), second))


def unpack_received(groups, table):
    low = lax.broadcasted_iota(jnp.int32, (TABLE, HALF), 1) < SLOTS
    for pair in range(2):
        lanes = slice(pair * HALF, pair * HALF + HALF)
        first = groups[2 * pair]
        second = groups[2 * pair + 1]
        for n, value in enumerate(
            (
                jnp.where(low, first, pltpu.roll(second, SLOTS, 1)),
                jnp.where(low, pltpu.roll(first, SLOTS, 1), second),
            )
        ):
            hi, lo = split(value)
            table[n * 2 * TABLE : n * 2 * TABLE + TABLE, lanes] = hi
            table[n * 2 * TABLE + TABLE : n * 2 * TABLE + 2 * TABLE, lanes] = lo


def one_hot(codes, first, rows):
    ids = lax.broadcasted_iota(jnp.int32, (rows, codes.shape[1]), 0) + first
    return jnp.where(ids == codes, 1.0, 0.0).astype(BF16)


def first_kernel(
    fwd,
    adj,
    star,
    stiffness,
    face_proj,
    send_element,
    send_face,
    face_kind,
    neighbor_index,
    neighbor_face,
    cluster,
    orientation,
    face_lift,
    face_orient,
    flux_local,
    flux_neighbor,
    derived,
    pick_local,
    pick_remote,
    pick_send,
    take_fine,
    give_fine,
    fine_star,
    wstiff,
    wstiff_t,
    wproj,
    wlift,
    worient,
    star_kept,
    local_kept,
    neighbor_kept,
    kind_kept,
    turn_kept,
    cluster_kept,
    stage,
    x3,
    spread,
    codes,
    series,
    raw,
    local_picks,
    sems,
):
    copies = [
        pltpu.make_async_copy(source, kept, sems.at[2, i])
        for i, (source, kept) in enumerate(
            ((star, star_kept), (flux_local, local_kept), (flux_neighbor, neighbor_kept))
        )
    ]
    loads = [
        pltpu.make_async_copy(field, raw.at[n], sems.at[3, n]) for n, field in enumerate((fwd, adj))
    ]
    for copy in loads + copies:
        copy.start()
    star = star_kept
    kind_kept[...] = face_kind[...]
    turn_kept[...] = orientation[...]
    cluster_kept[...] = cluster[...]
    fill_stiff(wstiff, stage, stiffness, False)
    fill_stiff(wstiff_t, stage, stiffness, True)
    fill_proj(wproj, stage, face_proj)
    fill_lift(wlift, stage, face_lift)
    fill_orient(worient, stage, face_orient)

    send_code = send_face[...] * ELEMS + send_element[...]
    for g in range(4):
        codes[0:1, g * SLOTS : g * SLOTS + SLOTS] = send_code[g : g + 1]
    for block in range(4):
        rows = slice(block * ELEMS, block * ELEMS + ELEMS)
        pick_send[rows, :] = one_hot(codes[0:1, :], block * ELEMS, ELEMS)
    for f in range(4):
        lanes = slice(f * ELEMS, f * ELEMS + ELEMS)
        kind = face_kind[f : f + 1, :]
        index = neighbor_index[f : f + 1, :]
        local = jnp.where(kind == 0, neighbor_face[f : f + 1, :] * ELEMS + index, -1)
        remote = jnp.where(kind == 1, index, -1)
        for block in range(4):
            rows = slice(block * ELEMS, block * ELEMS + ELEMS)
            local_picks[rows, lanes] = one_hot(local, block * ELEMS, ELEMS)
        pick_remote[:, lanes] = one_hot(remote, 0, ELEMS)
    table_out = pltpu.make_async_copy(local_picks, pick_local, sems.at[3, 2])
    table_out.start()

    fine = cluster[...] == 0
    upper = lax.broadcasted_iota(jnp.int32, (ELEMS, ELEMS), 0) < lax.broadcasted_iota(
        jnp.int32, (ELEMS, ELEMS), 1
    )
    flags = jnp.broadcast_to(jnp.where(fine, 1.0, 0.0), (FROWS, ELEMS)).astype(BF16)
    rank = dot(flags, jnp.where(upper, 1.0, 0.0).astype(BF16))[0:1]
    place_of = jnp.where(fine, rank.astype(jnp.int32), -1)
    slot = lax.broadcasted_iota(jnp.int32, (HALF, ELEMS), 0)
    slot = jnp.where(slot < SLOTS, slot, slot - SLOTS)
    chosen = jnp.where(slot == place_of, 1.0, 0.0)
    pick_t = chosen.T.astype(BF16)
    below = lax.broadcasted_iota(jnp.int32, (HALF, ELEMS), 0) < SLOTS
    for n in range(2):
        own = jnp.where(below, chosen, 0.0) if n == 0 else jnp.where(below, 0.0, chosen)
        give_fine[n] = own.astype(BF16)
        take_fine[n] = own.T.astype(BF16)
    low1 = lax.broadcasted_iota(jnp.int32, (1, HALF), 1) < SLOTS
    copies[0].wait()
    for d in range(3):
        plain = []
        for q in range(QUANT):
            hi, lo = split(star[q, :, d, :])
            plain.append(dot(hi, pick_t) + dot(lo, pick_t))
        for q in range(QUANT):
            for p in range(QUANT):
                fine_star[q, p, d : d + 1, :] = jnp.where(
                    low1, plain[q][p : p + 1], plain[p][q : q + 1]
                )

    for n in range(2):
        loads[n].wait()
        for q in range(QUANT):
            series[0, n, q, 0:BASIS, :] = raw[n, q]
            series[0, n, q, BASIS:ROWS, :] = jnp.zeros((ROWS - BASIS, ELEMS), F32)

    def step(degree, _):
        for n in range(2):
            for q in range(QUANT):
                stack_split(x3, q, series[degree, n, q])
            for q in range(QUANT):
                spread[q] = dot(wstiff[...], x3[q])
            for half in range(2):

                def emit(q, lanes, value):
                    series[degree + 1, n, q, :, lanes] = value

                star_apply(spread, star, n == 1, half, emit)
        for n in range(2):
            pltpu.make_async_copy(
                series.at[degree + 1, n], derived.at[n, degree], sems.at[n, degree]
            ).start()
        return 0

    lax.fori_loop(0, ORDER - 1, step, 0)
    copies[1].wait()
    copies[2].wait()
    table_out.wait()
    for n in range(2):
        for degree in range(ORDER - 1):
            pltpu.make_async_copy(
                series.at[degree + 1, n], derived.at[n, degree], sems.at[n, degree]
            ).wait()


def weights_of(smallest):
    dt = 0.5 * smallest
    early = []
    late = []
    power = dt
    for degree in range(ORDER):
        scale = 1.0 / math.factorial(degree + 1)
        early.append(power * scale)
        late.append(power * (scale * (2.0 ** (degree + 1) - 1.0)))
        power = power * dt
    return early, late


def integral_kernel(
    steps,
    fwd,
    adj,
    derived,
    pick_send,
    wproj,
    out0,
    out1,
    out2,
    out3,
    integral,
    faces,
    table,
    x3,
    series,
    start,
    least,
    sems,
):
    outs = (out0, out1, out2, out3)
    third = QUANT // 3
    starts = []
    copies = []
    for n, field in enumerate((fwd, adj)):
        starts.append(pltpu.make_async_copy(field, start.at[n], sems.at[n, 3]))
        starts[n].start()
        copies.append([])
        for part in range(3):
            some = slice(part * third, part * third + third)
            copies[n].append(
                pltpu.make_async_copy(
                    derived.at[n, :, some], series.at[n, :, some], sems.at[n, part]
                )
            )
            copies[n][part].start()
    smallest = jnp.min(steps[...])
    least[...] = jnp.full(least.shape, smallest, F32)
    early, _ = weights_of(smallest)
    for n in range(2):
        starts[n].wait()
        for q in range(QUANT):
            if q % third == 0:
                copies[n][q // third].wait()
            integral[n, q, 0:BASIS, :] = early[0] * start[n, q]
            integral[n, q, BASIS:ROWS, :] = jnp.zeros((ROWS - BASIS, ELEMS), F32)
            total = integral[n, q]
            for degree in range(1, ORDER):
                total = total + early[degree] * series[n, degree - 1, q]
            integral[n, q] = total
            stack_split(x3.at[n], q, total)
        project(x3.at[n], wproj, table, n, faces)

    def send(g, value):
        outs[g][...] = value

    pack_send(table, pick_send, send)


def flux_apply(source, weights, adjoint, n, f, half, acc):
    lanes = slice(half * HALF, half * HALF + HALF)
    rows = slice(f * FROWS, f * FROWS + FROWS)
    for p in range(QUANT):
        value = source[n, p, rows, lanes]
        for q in range(QUANT):
            if adjoint:
                weight = weights[p, q, f : f + 1, lanes]
            else:
                weight = weights[q, p, f : f + 1, lanes]
            term = value * weight
            acc[q] = term if acc[q] is None else acc[q] + term
    return acc


def local_part(
    x3, wstiff_t, spread, star, faces, table, flux_local, pick_local, volume, flux_sum, gathered
):
    for n in range(2):
        for q in range(QUANT):
            spread[q] = dot(wstiff_t[...], x3[n, q])
        for half in range(2):

            def emit(q, lanes, value):
                volume[n, q, :, lanes] = value

            star_apply(spread, star, n == 1, half, emit)
    for f in range(4):
        lanes = slice(f * ELEMS, f * ELEMS + ELEMS)
        found = dot(table[...], pick_local[:, lanes])
        for n in range(2):
            gathered[n, f] = (
                found[n * 2 * TABLE : n * 2 * TABLE + TABLE]
                + found[n * 2 * TABLE + TABLE : n * 2 * TABLE + 2 * TABLE]
            )
    for n in range(2):
        for f in range(4):
            for half in range(2):
                acc = flux_apply(faces, flux_local, n == 1, n, f, half, [None] * QUANT)
                for q in range(QUANT):
                    flux_sum[
                        n,
                        q,
                        f * FROWS : f * FROWS + FROWS,
                        half * HALF : half * HALF + HALF,
                    ] = acc[q]


def remote_part(
    groups,
    rtable,
    pick_remote,
    gathered,
    faces,
    face_kind,
    orientation,
    worient,
    x3o,
    other,
    flux_sum,
    flux_neighbor,
    x3l,
    wlift,
    volume,
    emit,
):
    unpack_received(groups, rtable)
    for f in range(4):
        lanes = slice(f * ELEMS, f * ELEMS + ELEMS)
        rows = slice(f * FROWS, f * FROWS + FROWS)
        found = dot(rtable[...], pick_remote[:, lanes])
        turn = orientation[f : f + 1, :]
        surface = face_kind[f : f + 1, :] == 2
        for n in range(2):
            total = (
                found[n * 2 * TABLE : n * 2 * TABLE + TABLE]
                + found[n * 2 * TABLE + TABLE : n * 2 * TABLE + 2 * TABLE]
                + gathered[n, f]
            )
            hi, lo = split(total)
            for q in range(QUANT):
                part = slice(q * FROWS, q * FROWS + FROWS)
                x3o[n, f, q, 0:FROWS, :] = hi[part]
                x3o[n, f, q, FROWS : 2 * FROWS, :] = lo[part]
                x3o[n, f, q, 2 * FROWS : 3 * FROWS, :] = hi[part]
            for q in range(QUANT):
                three = dot(worient[...], x3o[n, f, q])
                turned = jnp.where(
                    turn == 0,
                    three[0:FROWS],
                    jnp.where(turn == 1, three[FROWS : 2 * FROWS], three[2 * FROWS : 3 * FROWS]),
                )
                own = faces[n, q, rows, :]
                if q in MIRRORED:
                    own = -own
                other[n, q, rows, :] = turned + jnp.where(surface, own, 0.0)
    for n in range(2):
        for f in range(4):
            rows = slice(f * FROWS, f * FROWS + FROWS)
            for half in range(2):
                lanes = slice(half * HALF, half * HALF + HALF)
                acc = [flux_sum[n, q, rows, lanes] for q in range(QUANT)]
                acc = flux_apply(other, flux_neighbor, n == 1, n, f, half, acc)
                for q in range(QUANT):
                    hi, lo = split(acc[q])
                    x3l[q, f * FROWS : f * FROWS + FROWS, lanes] = hi
                    x3l[q, (4 + f) * FROWS : (5 + f) * FROWS, lanes] = lo
                    x3l[q, (8 + f) * FROWS : (9 + f) * FROWS, lanes] = hi
        for q in range(QUANT):
            emit(n, q, volume[n, q] + dot(wlift[...], x3l[q]))


def middle_kernel(
    least,
    start,
    integral,
    later,
    in0,
    in1,
    in2,
    in3,
    pick_remote,
    pick_send,
    take_fine,
    give_fine,
    fine_star,
    gathered,
    faces,
    face_kind,
    orientation,
    worient,
    flux_sum,
    flux_neighbor,
    wlift,
    volume,
    cluster,
    wstiff,
    wproj,
    out0,
    out1,
    out2,
    out3,
    base,
    faces_out,
    table,
    x3,
    sens,
    rtable,
    x3o,
    other,
    x3l,
    wide,
    x3c,
    spread_c,
    fields_c,
):
    outs = (out0, out1, out2, out3)
    early, _ = weights_of(jnp.min(least[...]))
    x3c[QUANT // 2, :, HALF:] = jnp.zeros((3 * PACK, HALF), BF16)
    fine = cluster[...] == 0
    active = cluster[...] <= 1

    def emit_first(n, q, value):
        before = jnp.concatenate([start[n, q], jnp.zeros((ROWS - BASIS, ELEMS), F32)], 0)
        moved = before + value
        base[n, q] = jnp.where(active, moved, before)
        hi, lo = split(jnp.concatenate([moved, jnp.zeros((PACK - ROWS, ELEMS), F32)], 0))
        wide[q, :, 2 * n * ELEMS : (2 * n + 1) * ELEMS] = hi
        wide[q, :, (2 * n + 1) * ELEMS : (2 * n + 2) * ELEMS] = lo

    remote_part(
        [in0[...], in1[...], in2[...], in3[...]],
        rtable,
        pick_remote,
        gathered,
        faces,
        face_kind,
        orientation,
        worient,
        x3o,
        other,
        flux_sum,
        flux_neighbor,
        x3l,
        wlift,
        volume,
        emit_first,
    )

    for q in range(QUANT):
        value = jnp.zeros((ROWS, HALF), F32)
        for n in range(2):
            for part in range(2):
                lanes = slice((2 * n + part) * ELEMS, (2 * n + part + 1) * ELEMS)
                value = value + dot(wide[q, :, lanes], take_fine[n])[0:ROWS]
        fields_c[q] = early[0] * value
        stack_pair(x3c, q, value)
    for degree in range(1, ORDER):
        for pair in range((QUANT + 1) // 2):
            spread_c[pair] = dot(wstiff[...], x3c[pair])
        acc = [None] * QUANT
        for p in range(QUANT):
            side = slice(p % 2 * HALF, p % 2 * HALF + HALF)
            for d in range(3):
                value = spread_c[p // 2, d * ROWS : d * ROWS + ROWS, side]
                for q in range(QUANT):
                    term = value * fine_star[q, p, d : d + 1, :]
                    acc[q] = term if acc[q] is None else acc[q] + term
        for q in range(QUANT):
            fields_c[q] = fields_c[q] + early[degree] * acc[q]
            if degree < ORDER - 1:
                stack_pair(x3c, q, acc[q])

    products = jnp.zeros((ROWS, ELEMS), F32)
    for q in range(QUANT):
        hi, lo = split(jnp.concatenate([fields_c[q], jnp.zeros((PACK - ROWS, HALF), F32)], 0))
        both = []
        for n in range(2):
            renewed = (dot(hi, give_fine[n]) + dot(lo, give_fine[n]))[0:ROWS]
            value = jnp.where(fine, renewed, later[n, q])
            stack_split(x3.at[n], q, value)
            both.append(value)
        products = products + integral[0, q] * integral[1, q] + both[0] * both[1]
    sens[...] = jnp.sum(products, axis=0, keepdims=True)
    for n in range(2):
        project(x3.at[n], wproj, table, n, faces_out)

    def send(g, value):
        outs[g][...] = value

    pack_send(table, pick_send, send)


def local_kernel(
    x3, star, faces, table, flux_local, pick_local, wstiff_t, volume, flux_sum, gathered, spread
):
    local_part(
        x3, wstiff_t, spread, star, faces, table, flux_local, pick_local, volume, flux_sum, gathered
    )


def first_local_kernel(
    x3,
    star,
    faces,
    table,
    flux_local,
    pick_local,
    wstiff_t,
    least,
    start,
    series,
    volume,
    flux_sum,
    gathered,
    later,
    spread,
):
    local_part(
        x3, wstiff_t, spread, star, faces, table, flux_local, pick_local, volume, flux_sum, gathered
    )
    _, late = weights_of(jnp.min(least[...]))
    for n in range(2):
        for q in range(QUANT):
            later[n, q, 0:BASIS, :] = late[0] * start[n, q]
            later[n, q, BASIS:ROWS, :] = jnp.zeros((ROWS - BASIS, ELEMS), F32)
            total = later[n, q]
            for degree in range(1, ORDER):
                total = total + late[degree] * series[n, degree - 1, q]
            later[n, q] = total


def last_kernel(
    in0,
    in1,
    in2,
    in3,
    pick_remote,
    gathered,
    faces,
    face_kind,
    orientation,
    worient,
    flux_sum,
    flux_neighbor,
    wlift,
    volume,
    base,
    cluster,
    sens,
    fwd,
    adj,
    sens_out,
    final,
    sems,
    rtable,
    x3o,
    other,
    x3l,
):
    active = cluster[...] <= 1
    copies = [
        pltpu.make_async_copy(final.at[n], out, sems.at[n]) for n, out in enumerate((fwd, adj))
    ]
    copies.append(pltpu.make_async_copy(sens, sens_out, sems.at[2]))
    copies[2].start()

    def emit(n, q, value):
        done = base[n, q] + jnp.where(active, value, 0.0)
        final[n, q] = done[0:BASIS]
        if q == QUANT - 1:
            copies[n].start()

    remote_part(
        [in0[...], in1[...], in2[...], in3[...]],
        rtable,
        pick_remote,
        gathered,
        faces,
        face_kind,
        orientation,
        worient,
        x3o,
        other,
        flux_sum,
        flux_neighbor,
        x3l,
        wlift,
        volume,
        emit,
    )
    for copy in copies:
        copy.wait()


def call(kernel, args, outs, scratch, flops, spaces=None, out_spaces=None, far=()):
    whole = pl.BlockSpec(memory_space=pltpu.VMEM)
    spaces = spaces or {}
    out_spaces = out_spaces or {}
    args = [
        pltpu.with_memory_space_constraint(x, pltpu.HBM if i in far else pltpu.VMEM)
        for i, x in enumerate(args)
    ]
    return pl.pallas_call(
        kernel,
        out_shape=outs,
        in_specs=[spaces.get(i, whole) for i in range(len(args))],
        out_specs=tuple(out_spaces.get(i, whole) for i in range(len(outs))),
        scratch_shapes=scratch,
        compiler_params=pltpu.CompilerParams(vmem_limit_bytes=VMEM_LIMIT),
        cost_estimate=pl.CostEstimate(flops=flops, bytes_accessed=4000000, transcendentals=0),
    )(*args)


def keep(*shape, dtype=F32):
    return pltpu.VMEM(shape, dtype)


def deliver(outgoing):
    received = []
    for value, by in zip(outgoing, (2, 1, -1, -2)):
        length = lax.axis_size("dom")
        pairs = [(i, (i + by) % length) for i in range(length)]
        received.append(lax.ppermute(value, "dom", pairs))
    return received


def shards(
    fwd_dofs,
    adj_dofs,
    star,
    flux_local,
    flux_neighbor,
    timescale,
    cluster,
    face_kind,
    neighbor_index,
    neighbor_face,
    orientation,
    send_element,
    send_face,
    stiffness,
    face_proj,
    face_lift,
    face_orient,
):
    count = lax.axis_size("dom")
    steps = lax.all_to_all(jnp.broadcast_to(timescale, (count, 1, ELEMS)), "dom", 0, 0)
    cluster = cluster.reshape(1, ELEMS)

    fwd_dofs = jnp.transpose(fwd_dofs, (1, 0, 2))
    adj_dofs = jnp.transpose(adj_dofs, (1, 0, 2))
    star = jnp.transpose(star, (1, 2, 0, 3))
    flux_local = jnp.transpose(flux_local, (1, 2, 0, 3))
    flux_neighbor = jnp.transpose(flux_neighbor, (1, 2, 0, 3))
    face_proj = jnp.transpose(face_proj, (1, 0, 2))
    face_lift = jnp.transpose(face_lift, (2, 0, 1))

    bf16 = {"dtype": BF16}
    whole = pl.BlockSpec(memory_space=pltpu.VMEM)
    away = pl.BlockSpec(memory_space=pl.ANY)
    message = keep(TABLE, HALF)
    face_data = keep(2, QUANT, 4 * FROWS, ELEMS)
    table_data = keep(4 * TABLE, 4 * ELEMS, **bf16)
    stacked = keep(2, QUANT, 3 * PACK, ELEMS, **bf16)
    fields = keep(2, QUANT, ROWS, ELEMS)
    apart = (2, ORDER - 1, QUANT, ROWS, ELEMS)
    spread = keep(QUANT, 3 * ROWS, ELEMS)
    remote_scratch = (
        keep(4 * TABLE, ELEMS, **bf16),
        keep(2, 4, QUANT, 3 * FROWS, ELEMS, **bf16),
        face_data,
        keep(QUANT, 12 * FROWS, ELEMS, **bf16),
    )

    (
        derived,
        pick_local,
        pick_remote,
        pick_send,
        take_fine,
        give_fine,
        fine_star,
        wstiff,
        wstiff_t,
        wproj,
        wlift,
        worient,
        star,
        flux_local,
        flux_neighbor,
        face_kind,
        orientation,
        cluster,
    ) = call(
        first_kernel,
        (
            fwd_dofs,
            adj_dofs,
            star,
            stiffness,
            face_proj,
            send_element,
            send_face,
            face_kind,
            neighbor_index,
            neighbor_face,
            cluster,
            orientation,
            face_lift,
            face_orient,
            flux_local,
            flux_neighbor,
        ),
        (
            pltpu.HBM(apart, F32),
            pltpu.HBM((4 * ELEMS, 4 * ELEMS), BF16),
            keep(ELEMS, 4 * ELEMS, **bf16),
            keep(4 * ELEMS, ELEMS, **bf16),
            keep(2, ELEMS, HALF, **bf16),
            keep(2, HALF, ELEMS, **bf16),
            keep(QUANT, QUANT, 3, HALF),
            keep(3 * ROWS, 3 * PACK, **bf16),
            keep(3 * ROWS, 3 * PACK, **bf16),
            keep(4 * FROWS, 3 * PACK, **bf16),
            keep(ROWS, 12 * FROWS, **bf16),
            keep(3 * FROWS, 3 * FROWS, **bf16),
            keep(*star.shape),
            keep(*flux_local.shape),
            keep(*flux_neighbor.shape),
            keep(4, ELEMS, dtype=jnp.int32),
            keep(4, ELEMS, dtype=jnp.int32),
            keep(1, ELEMS, dtype=jnp.int32),
        ),
        (
            keep(128, 256),
            keep(QUANT, 3 * PACK, ELEMS, **bf16),
            spread,
            keep(8, ELEMS, dtype=jnp.int32),
            keep(ORDER, 2, QUANT, ROWS, ELEMS),
            keep(2, QUANT, BASIS, ELEMS),
            keep(4 * ELEMS, 4 * ELEMS, **bf16),
            pltpu.SemaphoreType.DMA((4, ORDER - 1)),
        ),
        14000000000,
        far=range(16),
        spaces={0: away, 1: away, 2: away, 14: away, 15: away},
        out_spaces={0: away, 1: away},
    )

    local_out = (fields, face_data, keep(2, 4, TABLE, ELEMS))
    *outgoing, integral, faces, table, x3, series, start, least = call(
        integral_kernel,
        (steps, fwd_dofs, adj_dofs, derived, pick_send, wproj),
        (message,) * 4
        + (
            fields,
            face_data,
            table_data,
            stacked,
            keep(*apart),
            keep(2, QUANT, BASIS, ELEMS),
            keep(8, HALF),
        ),
        (pltpu.SemaphoreType.DMA((2, 4)),),
        2000000000,
        spaces={1: away, 2: away, 3: away},
        far=(1, 2, 3),
    )
    received = deliver(outgoing)
    volume, flux_sum, gathered, later = call(
        first_local_kernel,
        (x3, star, faces, table, flux_local, pick_local, wstiff_t, least, start, series),
        local_out + (fields,),
        (spread,),
        4000000000,
    )

    *outgoing, base, faces, table, x3, sens = call(
        middle_kernel,
        (
            least,
            start,
            integral,
            later,
            *received,
            pick_remote,
            pick_send,
            take_fine,
            give_fine,
            fine_star,
            gathered,
            faces,
            face_kind,
            orientation,
            worient,
            flux_sum,
            flux_neighbor,
            wlift,
            volume,
            cluster,
            wstiff,
            wproj,
        ),
        (message,) * 4
        + (keep(2, QUANT, ROWS, ELEMS), face_data, table_data, stacked, keep(1, ELEMS)),
        remote_scratch
        + (
            keep(QUANT, PACK, 4 * ELEMS, **bf16),
            keep((QUANT + 1) // 2, 3 * PACK, ELEMS, **bf16),
            keep((QUANT + 1) // 2, 3 * ROWS, ELEMS),
            keep(QUANT, ROWS, HALF),
        ),
        8000000000,
    )
    received = deliver(outgoing)
    volume, flux_sum, gathered = call(
        local_kernel,
        (x3, star, faces, table, flux_local, pick_local, wstiff_t),
        local_out,
        (spread,),
        4000000000,
    )

    fwd_final, adj_final, sens = call(
        last_kernel,
        (
            *received,
            pick_remote,
            gathered,
            faces,
            face_kind,
            orientation,
            worient,
            flux_sum,
            flux_neighbor,
            wlift,
            volume,
            base,
            cluster,
            sens,
        ),
        (
            pltpu.HBM(fwd_dofs.shape, F32),
            pltpu.HBM(adj_dofs.shape, F32),
            pltpu.HBM((1, ELEMS), F32),
        ),
        (keep(2, QUANT, BASIS, ELEMS), pltpu.SemaphoreType.DMA((3,))) + remote_scratch,
        4000000000,
        out_spaces={0: away, 1: away, 2: away},
    )
    return (
        jnp.transpose(fwd_final, (1, 0, 2)),
        jnp.transpose(adj_final, (1, 0, 2)),
        sens.reshape(ELEMS),
    )


def solution(mesh):
    return jax.shard_map(
        shards,
        mesh=mesh,
        in_specs=(
            P(None, None, "dom"),
            P(None, None, "dom"),
            P(None, None, None, "dom"),
            P(None, None, None, "dom"),
            P(None, None, None, "dom"),
            P("dom"),
            P("dom"),
            P(None, "dom"),
            P(None, "dom"),
            P(None, "dom"),
            P(None, "dom"),
            P(None, "dom"),
            P(None, "dom"),
            P(),
            P(),
            P(),
            P(),
        ),
        out_specs=(P(None, None, "dom"), P(None, None, "dom"), P("dom")),
        check_vma=False,
    )
```

```python
import math

import jax
import jax.numpy as jnp
from jax import lax
from jax.experimental import pallas as pl
from jax.experimental.pallas import tpu as pltpu
from jax.sharding import PartitionSpec as P

BASIS = 35
FACE_BASIS = 15
QUANT = 9
ORDER = 5
ROWS = 40
PACK = 48
FROWS = 16
ELEMS = 256
SLOTS = 64
HALF = 128
TABLE = QUANT * FROWS
MIRRORED = (0, 3, 5)
F32 = jnp.float32
BF16 = jnp.bfloat16
VMEM_LIMIT = 16 * 1024 * 1024


def dot(a, b):
    return jnp.dot(a, b, preferred_element_type=F32)


def split(x):
    hi = x.astype(BF16)
    return hi, (x - hi.astype(F32)).astype(BF16)


def spread_columns(rows, cols, starts):
    gap = lax.broadcasted_iota(jnp.int32, (rows, cols), 1) - lax.broadcasted_iota(
        jnp.int32, (rows, cols), 0
    )
    mask = gap == starts[0]
    for start in starts[1:]:
        mask = mask | (gap == start)
    return jnp.where(mask, 1.0, 0.0).astype(BF16)


def fill(out, stage, mats, step, period):
    rows, cols = out.shape
    stage[...] = jnp.zeros(stage.shape, F32)
    for k, mat in enumerate(mats):
        stage[k * step : k * step + mat.shape[0], 0 : mat.shape[1]] = mat
    hi, lo = split(stage[0:rows, :])
    width = stage.shape[1]
    out[...] = (
        dot(hi, spread_columns(width, cols, (0, period)))
        + dot(lo, spread_columns(width, cols, (2 * period,)))
    ).astype(BF16)


def fill_lift(out, face_lift):
    total = None
    for f in range(4):
        hi, lo = split(face_lift[:, f, :].T)
        base = f * FROWS
        part = dot(
            hi, spread_columns(FACE_BASIS, 12 * FROWS, (base, 4 * FROWS + base))
        ) + dot(lo, spread_columns(FACE_BASIS, 12 * FROWS, (8 * FROWS + base,)))
        total = part if total is None else total + part
    out[...] = jnp.concatenate([total, jnp.zeros((ROWS - BASIS, 12 * FROWS), F32)], 0).astype(BF16)


def stack_split(x3, q, x):
    hi, lo = split(jnp.concatenate([x, jnp.zeros((PACK - ROWS, x.shape[1]), F32)], 0))
    x3[q, 0:PACK, :] = hi
    x3[q, PACK : 2 * PACK, :] = lo
    x3[q, 2 * PACK : 3 * PACK, :] = hi


def stack_pair(x3, q, x):
    hi, lo = split(jnp.concatenate([x, jnp.zeros((PACK - ROWS, HALF), F32)], 0))
    lanes = slice(q % 2 * HALF, q % 2 * HALF + HALF)
    x3[q // 2, 0:PACK, lanes] = hi
    x3[q // 2, PACK : 2 * PACK, lanes] = lo
    x3[q // 2, 2 * PACK : 3 * PACK, lanes] = hi


def star_apply(spread, star, adjoint, half, emit):
    lanes = slice(half * HALF, half * HALF + HALF)
    acc = [None] * QUANT
    for p in range(QUANT):
        for d in range(3):
            value = spread[p, d * ROWS : d * ROWS + ROWS, lanes]
            for q in range(QUANT):
                if adjoint:
                    weight = star[p, q, d : d + 1, lanes]
                else:
                    weight = star[q, p, d : d + 1, lanes]
                term = value * weight
                acc[q] = term if acc[q] is None else acc[q] + term
    for q in range(QUANT):
        emit(q, lanes, acc[q])


def project(x3, wproj, table, n, faces=None):
    for q in range(QUANT):
        value = dot(wproj[...], x3[q])
        if faces is not None:
            faces[n, q] = value
        hi, lo = split(value)
        for f in range(4):
            lanes = slice(f * ELEMS, f * ELEMS + ELEMS)
            rows = slice(f * FROWS, f * FROWS + FROWS)
            base = n * 2 * TABLE + q * FROWS
            table[base : base + FROWS, lanes] = hi[rows]
            table[base + TABLE : base + TABLE + FROWS, lanes] = lo[rows]


def pack_send(table, pick, emit):
    found = dot(table[...], pick[...])
    low = lax.broadcasted_iota(jnp.int32, (TABLE, HALF), 1) < SLOTS
    sides = [
        found[n * 2 * TABLE : n * 2 * TABLE + TABLE]
        + found[n * 2 * TABLE + TABLE : n * 2 * TABLE + 2 * TABLE]
        for n in range(2)
    ]
    for pair in range(2):
        lanes = slice(pair * HALF, pair * HALF + HALF)
        first = sides[0][:, lanes]
        second = sides[1][:, lanes]
        emit(2 * pair, jnp.where(low, first, pltpu.roll(second, SLOTS, 1)))
        emit(2 * pair + 1, jnp.where(low, pltpu.roll(first, SLOTS, 1), second))


def unpack_received(groups, table):
    low = lax.broadcasted_iota(jnp.int32, (TABLE, HALF), 1) < SLOTS
    for pair in range(2):
        lanes = slice(pair * HALF, pair * HALF + HALF)
        first = groups[2 * pair]
        second = groups[2 * pair + 1]
        for n, value in enumerate(
            (
                jnp.where(low, first, pltpu.roll(second, SLOTS, 1)),
                jnp.where(low, pltpu.roll(first, SLOTS, 1), second),
            )
        ):
            hi, lo = split(value)
            table[n * 2 * TABLE : n * 2 * TABLE + TABLE, lanes] = hi
            table[n * 2 * TABLE + TABLE : n * 2 * TABLE + 2 * TABLE, lanes] = lo


def one_hot(codes, first, rows):
    ids = lax.broadcasted_iota(jnp.int32, (rows, codes.shape[1]), 0) + first
    return jnp.where(ids == codes, 1.0, 0.0).astype(BF16)


def first_kernel(
    fwd,
    adj,
    star,
    stiffness,
    face_proj,
    send_element,
    send_face,
    face_kind,
    neighbor_index,
    neighbor_face,
    cluster,
    orientation,
    face_lift,
    face_orient,
    flux_local,
    derived,
    last,
    pick_local,
    pick_remote,
    pick_send,
    take_fine,
    give_fine,
    fine_star,
    wstiff,
    wstiff_t,
    wproj,
    wlift,
    worient,
    star_kept,
    local_kept,
    kind_kept,
    turn_kept,
    cluster_kept,
    stage,
    x3,
    spread,
    codes,
    series,
    raw,
    local_picks,
    star_rows,
    found,
    sems,
):
    copies = [
        pltpu.make_async_copy(source, kept, sems.at[2, i])
        for i, (source, kept) in enumerate(
            ((star, star_kept), (flux_local, local_kept))
        )
    ]
    loads = [
        pltpu.make_async_copy(field, raw.at[n], sems.at[3, n]) for n, field in enumerate((fwd, adj))
    ]
    for copy in loads + copies:
        copy.start()
    star = star_kept
    kind_kept[...] = face_kind[...]
    turn_kept[...] = orientation[...]
    cluster_kept[...] = cluster[...]
    fill(wstiff, stage.at[0], [stiffness[d] for d in range(3)], ROWS, PACK)
    fill(wstiff_t, stage.at[1], [stiffness[d].T for d in range(3)], ROWS, PACK)
    fill(wproj, stage.at[2], [face_proj[:, f, :] for f in range(4)], FROWS, PACK)
    fill(worient, stage.at[3], [face_orient[o] for o in range(3)], FROWS, FROWS)
    fill_lift(wlift, face_lift)

    send_code = send_face[...] * ELEMS + send_element[...]
    for g in range(4):
        codes[0:1, g * SLOTS : g * SLOTS + SLOTS] = send_code[g : g + 1]
    for block in range(4):
        rows = slice(block * ELEMS, block * ELEMS + ELEMS)
        pick_send[rows, :] = one_hot(codes[0:1, :], block * ELEMS, ELEMS)
    for f in range(4):
        lanes = slice(f * ELEMS, f * ELEMS + ELEMS)
        kind = face_kind[f : f + 1, :]
        index = neighbor_index[f : f + 1, :]
        local = jnp.where(kind == 0, neighbor_face[f : f + 1, :] * ELEMS + index, -1)
        remote = jnp.where(kind == 1, index, -1)
        for block in range(4):
            rows = slice(block * ELEMS, block * ELEMS + ELEMS)
            local_picks[rows, lanes] = one_hot(local, block * ELEMS, ELEMS)
        pick_remote[:, lanes] = one_hot(remote, 0, ELEMS)
    table_out = pltpu.make_async_copy(local_picks, pick_local, sems.at[3, 2])
    table_out.start()

    fine = cluster[...] == 0
    upper = lax.broadcasted_iota(jnp.int32, (ELEMS, ELEMS), 0) < lax.broadcasted_iota(
        jnp.int32, (ELEMS, ELEMS), 1
    )
    flags = jnp.broadcast_to(jnp.where(fine, 1.0, 0.0), (FROWS, ELEMS)).astype(BF16)
    rank = dot(flags, jnp.where(upper, 1.0, 0.0).astype(BF16))[0:1]
    place_of = jnp.where(fine, rank.astype(jnp.int32), -1)
    slot = lax.broadcasted_iota(jnp.int32, (HALF, ELEMS), 0)
    slot = jnp.where(slot < SLOTS, slot, slot - SLOTS)
    chosen = jnp.where(slot == place_of, 1.0, 0.0)
    below = lax.broadcasted_iota(jnp.int32, (HALF, ELEMS), 0) < SLOTS
    for n in range(2):
        own = jnp.where(below, chosen, 0.0) if n == 0 else jnp.where(below, 0.0, chosen)
        give_fine[n] = own.astype(BF16)
        take_fine[n] = own.T.astype(BF16)
    copies[0].wait()
    for q in range(QUANT):
        for p in range(QUANT):
            base = 4 * (q * QUANT + p)
            star_rows[base : base + 3, :] = star[q, p]
    hi, lo = split(star_rows[...])
    take = chosen.T.astype(BF16)
    found[...] = dot(hi, take) + dot(lo, take)
    low1 = lax.broadcasted_iota(jnp.int32, (3, HALF), 1) < SLOTS
    for q in range(QUANT):
        for p in range(QUANT):
            plain = 4 * (q * QUANT + p)
            swapped = 4 * (p * QUANT + q)
            fine_star[q, p] = jnp.where(
                low1, found[plain : plain + 3, :], found[swapped : swapped + 3, :]
            )

    for n in range(2):
        loads[n].wait()
        for q in range(QUANT):
            series[0, n, q, 0:BASIS, :] = raw[n, q]
            series[0, n, q, BASIS:ROWS, :] = jnp.zeros((ROWS - BASIS, ELEMS), F32)

    def step(degree, write):
        for n in range(2):
            for q in range(QUANT):
                stack_split(x3, q, series[degree, n, q])
            for q in range(QUANT):
                spread[q] = dot(wstiff[...], x3[q])
            for half in range(2):

                def emit(q, lanes, value):
                    write(n, q, lanes, value)

                star_apply(spread, star, n == 1, half, emit)

    def stored(degree, n):
        return pltpu.make_async_copy(
            series.at[degree + 1, n], derived.at[n, degree], sems.at[n, degree]
        )

    def early_step(degree, _):
        def write(n, q, lanes, value):
            series[degree + 1, n, q, :, lanes] = value

        step(degree, write)
        for n in range(2):
            stored(degree, n).start()
        return 0

    def write_last(n, q, lanes, value):
        last[n, q, :, lanes] = value

    lax.fori_loop(0, ORDER - 2, early_step, 0)
    step(ORDER - 2, write_last)
    copies[1].wait()
    table_out.wait()
    for n in range(2):
        for degree in range(ORDER - 2):
            stored(degree, n).wait()


def weights_of(smallest):
    dt = 0.5 * smallest
    early = []
    late = []
    power = dt
    for degree in range(ORDER):
        scale = 1.0 / math.factorial(degree + 1)
        early.append(power * scale)
        late.append(power * (scale * (2.0 ** (degree + 1) - 1.0)))
        power = power * dt
    return early, late


def integral_kernel(
    steps,
    fwd,
    adj,
    derived,
    last,
    pick_send,
    wproj,
    flux_neighbor,
    out0,
    out1,
    out2,
    out3,
    integral,
    faces,
    table,
    x3,
    series,
    start,
    least,
    neighbor_kept,
    sems,
):
    outs = (out0, out1, out2, out3)
    third = QUANT // 3
    starts = []
    copies = []
    for n, field in enumerate((fwd, adj)):
        starts.append(pltpu.make_async_copy(field, start.at[n], sems.at[n, 3]))
        starts[n].start()
        copies.append([])
        for part in range(3):
            some = slice(part * third, part * third + third)
            copies[n].append(
                pltpu.make_async_copy(
                    derived.at[n, :, some], series.at[n, :, some], sems.at[n, part]
                )
            )
            copies[n][part].start()
    keeping = pltpu.make_async_copy(flux_neighbor, neighbor_kept, sems.at[2, 0])
    keeping.start()
    smallest = jnp.min(steps[...])
    least[...] = jnp.full(least.shape, smallest, F32)
    early, _ = weights_of(smallest)
    for n in range(2):
        starts[n].wait()
        for q in range(QUANT):
            if q % third == 0:
                copies[n][q // third].wait()
            integral[n, q, 0:BASIS, :] = early[0] * start[n, q]
            integral[n, q, BASIS:ROWS, :] = jnp.zeros((ROWS - BASIS, ELEMS), F32)
            total = integral[n, q] + early[ORDER - 1] * last[n, q]
            for degree in range(1, ORDER - 1):
                total = total + early[degree] * series[n, degree - 1, q]
            integral[n, q] = total
            stack_split(x3.at[n], q, total)
        project(x3.at[n], wproj, table, n, faces)

    def send(g, value):
        outs[g][...] = value

    pack_send(table, pick_send, send)
    keeping.wait()


def flux_apply(source, weights, adjoint, n, f, half, acc):
    lanes = slice(half * HALF, half * HALF + HALF)
    rows = slice(f * FROWS, f * FROWS + FROWS)
    for p in range(QUANT):
        value = source[n, p, rows, lanes]
        for q in range(QUANT):
            if adjoint:
                weight = weights[p, q, f : f + 1, lanes]
            else:
                weight = weights[q, p, f : f + 1, lanes]
            term = value * weight
            acc[q] = term if acc[q] is None else acc[q] + term
    return acc


def local_part(
    x3, wstiff_t, spread, star, faces, table, flux_local, pick_local, volume, flux_sum, gathered
):
    for n in range(2):
        for q in range(QUANT):
            spread[q] = dot(wstiff_t[...], x3[n, q])
        for half in range(2):

            def emit(q, lanes, value):
                volume[n, q, :, lanes] = value

            star_apply(spread, star, n == 1, half, emit)
    for f in range(4):
        lanes = slice(f * ELEMS, f * ELEMS + ELEMS)
        found = dot(table[...], pick_local[:, lanes])
        for n in range(2):
            gathered[n, f] = (
                found[n * 2 * TABLE : n * 2 * TABLE + TABLE]
                + found[n * 2 * TABLE + TABLE : n * 2 * TABLE + 2 * TABLE]
            )
    for n in range(2):
        for f in range(4):
            for half in range(2):
                acc = flux_apply(faces, flux_local, n == 1, n, f, half, [None] * QUANT)
                for q in range(QUANT):
                    flux_sum[
                        n,
                        q,
                        f * FROWS : f * FROWS + FROWS,
                        half * HALF : half * HALF + HALF,
                    ] = acc[q]


def remote_part(
    groups,
    rtable,
    pick_remote,
    gathered,
    faces,
    face_kind,
    orientation,
    worient,
    x3o,
    other,
    flux_sum,
    flux_neighbor,
    x3l,
    wlift,
    volume,
    emit,
):
    unpack_received(groups, rtable)
    for f in range(4):
        lanes = slice(f * ELEMS, f * ELEMS + ELEMS)
        rows = slice(f * FROWS, f * FROWS + FROWS)
        found = dot(rtable[...], pick_remote[:, lanes])
        turn = orientation[f : f + 1, :]
        surface = face_kind[f : f + 1, :] == 2
        for n in range(2):
            total = (
                found[n * 2 * TABLE : n * 2 * TABLE + TABLE]
                + found[n * 2 * TABLE + TABLE : n * 2 * TABLE + 2 * TABLE]
                + gathered[n, f]
            )
            hi, lo = split(total)
            for q in range(QUANT):
                part = slice(q * FROWS, q * FROWS + FROWS)
                x3o[n, f, q, 0:FROWS, :] = hi[part]
                x3o[n, f, q, FROWS : 2 * FROWS, :] = lo[part]
                x3o[n, f, q, 2 * FROWS : 3 * FROWS, :] = hi[part]
            for q in range(QUANT):
                three = dot(worient[...], x3o[n, f, q])
                turned = jnp.where(
                    turn == 0,
                    three[0:FROWS],
                    jnp.where(turn == 1, three[FROWS : 2 * FROWS], three[2 * FROWS : 3 * FROWS]),
                )
                own = faces[n, q, rows, :]
                if q in MIRRORED:
                    own = -own
                other[n, q, rows, :] = turned + jnp.where(surface, own, 0.0)
    for n in range(2):
        for f in range(4):
            rows = slice(f * FROWS, f * FROWS + FROWS)
            for half in range(2):
                lanes = slice(half * HALF, half * HALF + HALF)
                acc = [flux_sum[n, q, rows, lanes] for q in range(QUANT)]
                acc = flux_apply(other, flux_neighbor, n == 1, n, f, half, acc)
                for q in range(QUANT):
                    hi, lo = split(acc[q])
                    x3l[q, f * FROWS : f * FROWS + FROWS, lanes] = hi
                    x3l[q, (4 + f) * FROWS : (5 + f) * FROWS, lanes] = lo
                    x3l[q, (8 + f) * FROWS : (9 + f) * FROWS, lanes] = hi
        for q in range(QUANT):
            emit(n, q, volume[n, q] + dot(wlift[...], x3l[q]))


def middle_kernel(
    least,
    start,
    integral,
    later,
    in0,
    in1,
    in2,
    in3,
    pick_remote,
    pick_send,
    take_fine,
    give_fine,
    fine_star,
    gathered,
    faces,
    face_kind,
    orientation,
    worient,
    flux_sum,
    flux_neighbor,
    wlift,
    volume,
    cluster,
    wstiff,
    wproj,
    out0,
    out1,
    out2,
    out3,
    base,
    faces_out,
    table,
    x3,
    sens,
    rtable,
    x3o,
    other,
    x3l,
    wide,
    x3c,
    spread_c,
    fields_c,
):
    outs = (out0, out1, out2, out3)
    early, _ = weights_of(jnp.min(least[...]))
    x3c[QUANT // 2, :, HALF:] = jnp.zeros((3 * PACK, HALF), BF16)
    fine = cluster[...] == 0
    active = cluster[...] <= 1

    def emit_first(n, q, value):
        before = jnp.concatenate([start[n, q], jnp.zeros((ROWS - BASIS, ELEMS), F32)], 0)
        moved = before + value
        base[n, q] = jnp.where(active, moved, before)
        hi, lo = split(jnp.concatenate([moved, jnp.zeros((PACK - ROWS, ELEMS), F32)], 0))
        wide[q, :, 2 * n * ELEMS : (2 * n + 1) * ELEMS] = hi
        wide[q, :, (2 * n + 1) * ELEMS : (2 * n + 2) * ELEMS] = lo

    remote_part(
        [in0[...], in1[...], in2[...], in3[...]],
        rtable,
        pick_remote,
        gathered,
        faces,
        face_kind,
        orientation,
        worient,
        x3o,
        other,
        flux_sum,
        flux_neighbor,
        x3l,
        wlift,
        volume,
        emit_first,
    )

    for q in range(QUANT):
        value = jnp.zeros((ROWS, HALF), F32)
        for n in range(2):
            for part in range(2):
                lanes = slice((2 * n + part) * ELEMS, (2 * n + part + 1) * ELEMS)
                value = value + dot(wide[q, :, lanes], take_fine[n])[0:ROWS]
        fields_c[q] = early[0] * value
        stack_pair(x3c, q, value)
    for degree in range(1, ORDER):
        for pair in range((QUANT + 1) // 2):
            spread_c[pair] = dot(wstiff[...], x3c[pair])
        acc = [None] * QUANT
        for p in range(QUANT):
            side = slice(p % 2 * HALF, p % 2 * HALF + HALF)
            for d in range(3):
                value = spread_c[p // 2, d * ROWS : d * ROWS + ROWS, side]
                for q in range(QUANT):
                    term = value * fine_star[q, p, d : d + 1, :]
                    acc[q] = term if acc[q] is None else acc[q] + term
        for q in range(QUANT):
            fields_c[q] = fields_c[q] + early[degree] * acc[q]
            if degree < ORDER - 1:
                stack_pair(x3c, q, acc[q])

    products = jnp.zeros((ROWS, ELEMS), F32)
    for q in range(QUANT):
        hi, lo = split(jnp.concatenate([fields_c[q], jnp.zeros((PACK - ROWS, HALF), F32)], 0))
        both = []
        for n in range(2):
            renewed = (dot(hi, give_fine[n]) + dot(lo, give_fine[n]))[0:ROWS]
            value = jnp.where(fine, renewed, later[n, q])
            stack_split(x3.at[n], q, value)
            both.append(value)
        products = products + integral[0, q] * integral[1, q] + both[0] * both[1]
    sens[...] = jnp.sum(products, axis=0, keepdims=True)
    for n in range(2):
        project(x3.at[n], wproj, table, n, faces_out)

    def send(g, value):
        outs[g][...] = value

    pack_send(table, pick_send, send)


def local_kernel(
    x3, star, faces, table, flux_local, pick_local, wstiff_t, volume, flux_sum, gathered, spread
):
    local_part(
        x3, wstiff_t, spread, star, faces, table, flux_local, pick_local, volume, flux_sum, gathered
    )


def first_local_kernel(
    x3,
    star,
    faces,
    table,
    flux_local,
    pick_local,
    wstiff_t,
    least,
    start,
    series,
    last,
    volume,
    flux_sum,
    gathered,
    later,
    spread,
):
    local_part(
        x3, wstiff_t, spread, star, faces, table, flux_local, pick_local, volume, flux_sum, gathered
    )
    _, late = weights_of(jnp.min(least[...]))
    for n in range(2):
        for q in range(QUANT):
            later[n, q, 0:BASIS, :] = late[0] * start[n, q]
            later[n, q, BASIS:ROWS, :] = jnp.zeros((ROWS - BASIS, ELEMS), F32)
            total = later[n, q] + late[ORDER - 1] * last[n, q]
            for degree in range(1, ORDER - 1):
                total = total + late[degree] * series[n, degree - 1, q]
            later[n, q] = total


def last_kernel(
    in0,
    in1,
    in2,
    in3,
    pick_remote,
    gathered,
    faces,
    face_kind,
    orientation,
    worient,
    flux_sum,
    flux_neighbor,
    wlift,
    volume,
    base,
    cluster,
    sens,
    fwd,
    adj,
    sens_out,
    final,
    sems,
    rtable,
    x3o,
    other,
    x3l,
):
    active = cluster[...] <= 1
    copies = [
        pltpu.make_async_copy(final.at[n], out, sems.at[n]) for n, out in enumerate((fwd, adj))
    ]
    copies.append(pltpu.make_async_copy(sens, sens_out, sems.at[2]))
    copies[2].start()

    def emit(n, q, value):
        done = base[n, q] + jnp.where(active, value, 0.0)
        final[n, q] = done[0:BASIS]
        if q == QUANT - 1:
            copies[n].start()

    remote_part(
        [in0[...], in1[...], in2[...], in3[...]],
        rtable,
        pick_remote,
        gathered,
        faces,
        face_kind,
        orientation,
        worient,
        x3o,
        other,
        flux_sum,
        flux_neighbor,
        x3l,
        wlift,
        volume,
        emit,
    )
    for copy in copies:
        copy.wait()


def call(kernel, args, outs, scratch, flops, spaces=None, out_spaces=None, far=()):
    whole = pl.BlockSpec(memory_space=pltpu.VMEM)
    spaces = spaces or {}
    out_spaces = out_spaces or {}
    args = [
        pltpu.with_memory_space_constraint(x, pltpu.HBM if i in far else pltpu.VMEM)
        for i, x in enumerate(args)
    ]
    return pl.pallas_call(
        kernel,
        out_shape=outs,
        in_specs=[spaces.get(i, whole) for i in range(len(args))],
        out_specs=tuple(out_spaces.get(i, whole) for i in range(len(outs))),
        scratch_shapes=scratch,
        compiler_params=pltpu.CompilerParams(vmem_limit_bytes=VMEM_LIMIT),
        cost_estimate=pl.CostEstimate(flops=flops, bytes_accessed=4000000, transcendentals=0),
    )(*args)


def keep(*shape, dtype=F32):
    return pltpu.VMEM(shape, dtype)


def deliver(outgoing):
    received = []
    for value, by in zip(outgoing, (2, 1, -1, -2)):
        length = lax.axis_size("dom")
        pairs = [(i, (i + by) % length) for i in range(length)]
        received.append(lax.ppermute(value, "dom", pairs))
    return received


def shards(
    fwd_dofs,
    adj_dofs,
    star,
    flux_local,
    flux_neighbor,
    timescale,
    cluster,
    face_kind,
    neighbor_index,
    neighbor_face,
    orientation,
    send_element,
    send_face,
    stiffness,
    face_proj,
    face_lift,
    face_orient,
):
    count = lax.axis_size("dom")
    halves = jnp.minimum(timescale[:HALF], timescale[HALF:])
    steps = lax.all_to_all(jnp.broadcast_to(halves, (count, 1, HALF)), "dom", 0, 0)
    cluster = cluster.reshape(1, ELEMS)

    fwd_dofs = jnp.transpose(fwd_dofs, (1, 0, 2))
    adj_dofs = jnp.transpose(adj_dofs, (1, 0, 2))
    star = jnp.transpose(star, (1, 2, 0, 3))
    flux_local = jnp.transpose(flux_local, (1, 2, 0, 3))
    flux_neighbor = jnp.transpose(flux_neighbor, (1, 2, 0, 3))
    face_proj = jnp.transpose(face_proj, (1, 0, 2))
    face_lift = jnp.transpose(face_lift, (2, 0, 1))

    bf16 = {"dtype": BF16}
    whole = pl.BlockSpec(memory_space=pltpu.VMEM)
    away = pl.BlockSpec(memory_space=pl.ANY)
    message = keep(TABLE, HALF)
    face_data = keep(2, QUANT, 4 * FROWS, ELEMS)
    table_data = keep(4 * TABLE, 4 * ELEMS, **bf16)
    stacked = keep(2, QUANT, 3 * PACK, ELEMS, **bf16)
    fields = keep(2, QUANT, ROWS, ELEMS)
    apart = (2, ORDER - 2, QUANT, ROWS, ELEMS)
    spread = keep(QUANT, 3 * ROWS, ELEMS)
    remote_scratch = (
        keep(4 * TABLE, ELEMS, **bf16),
        keep(2, 4, QUANT, 3 * FROWS, ELEMS, **bf16),
        face_data,
        keep(QUANT, 12 * FROWS, ELEMS, **bf16),
    )

    (
        derived,
        last,
        pick_local,
        pick_remote,
        pick_send,
        take_fine,
        give_fine,
        fine_star,
        wstiff,
        wstiff_t,
        wproj,
        wlift,
        worient,
        star,
        flux_local,
        face_kind,
        orientation,
        cluster,
    ) = call(
        first_kernel,
        (
            fwd_dofs,
            adj_dofs,
            star,
            stiffness,
            face_proj,
            send_element,
            send_face,
            face_kind,
            neighbor_index,
            neighbor_face,
            cluster,
            orientation,
            face_lift,
            face_orient,
            flux_local,
        ),
        (
            pltpu.HBM(apart, F32),
            fields,
            pltpu.HBM((4 * ELEMS, 4 * ELEMS), BF16),
            keep(ELEMS, 4 * ELEMS, **bf16),
            keep(4 * ELEMS, ELEMS, **bf16),
            keep(2, ELEMS, HALF, **bf16),
            keep(2, HALF, ELEMS, **bf16),
            keep(QUANT, QUANT, 3, HALF),
            keep(3 * ROWS, 3 * PACK, **bf16),
            keep(3 * ROWS, 3 * PACK, **bf16),
            keep(4 * FROWS, 3 * PACK, **bf16),
            keep(ROWS, 12 * FROWS, **bf16),
            keep(3 * FROWS, 3 * FROWS, **bf16),
            keep(*star.shape),
            keep(*flux_local.shape),
            keep(4, ELEMS, dtype=jnp.int32),
            keep(4, ELEMS, dtype=jnp.int32),
            keep(1, ELEMS, dtype=jnp.int32),
        ),
        (
            keep(4, 128, 128),
            keep(QUANT, 3 * PACK, ELEMS, **bf16),
            spread,
            keep(8, ELEMS, dtype=jnp.int32),
            keep(ORDER - 1, 2, QUANT, ROWS, ELEMS),
            keep(2, QUANT, BASIS, ELEMS),
            keep(4 * ELEMS, 4 * ELEMS, **bf16),
            keep(336, ELEMS),
            keep(336, HALF),
            pltpu.SemaphoreType.DMA((4, ORDER - 1)),
        ),
        14000000000,
        far=range(15),
        spaces={0: away, 1: away, 2: away, 14: away},
        out_spaces={0: away, 2: away},
    )

    local_out = (fields, face_data, keep(2, 4, TABLE, ELEMS))
    *outgoing, integral, faces, table, x3, series, start, least, flux_neighbor = call(
        integral_kernel,
        (steps, fwd_dofs, adj_dofs, derived, last, pick_send, wproj, flux_neighbor),
        (message,) * 4
        + (
            fields,
            face_data,
            table_data,
            stacked,
            keep(*apart),
            keep(2, QUANT, BASIS, ELEMS),
            keep(8, HALF),
            keep(*flux_neighbor.shape),
        ),
        (pltpu.SemaphoreType.DMA((3, 4)),),
        2000000000,
        spaces={1: away, 2: away, 3: away, 7: away},
        far=(1, 2, 3, 7),
    )
    received = deliver(outgoing)
    volume, flux_sum, gathered, later = call(
        first_local_kernel,
        (x3, star, faces, table, flux_local, pick_local, wstiff_t, least, start, series, last),
        local_out + (fields,),
        (spread,),
        4000000000,
    )

    *outgoing, base, faces, table, x3, sens = call(
        middle_kernel,
        (
            least,
            start,
            integral,
            later,
            *received,
            pick_remote,
            pick_send,
            take_fine,
            give_fine,
            fine_star,
            gathered,
            faces,
            face_kind,
            orientation,
            worient,
            flux_sum,
            flux_neighbor,
            wlift,
            volume,
            cluster,
            wstiff,
            wproj,
        ),
        (message,) * 4
        + (keep(2, QUANT, ROWS, ELEMS), face_data, table_data, stacked, keep(1, ELEMS)),
        remote_scratch
        + (
            keep(QUANT, PACK, 4 * ELEMS, **bf16),
            keep((QUANT + 1) // 2, 3 * PACK, ELEMS, **bf16),
            keep((QUANT + 1) // 2, 3 * ROWS, ELEMS),
            keep(QUANT, ROWS, HALF),
        ),
        8000000000,
    )
    received = deliver(outgoing)
    volume, flux_sum, gathered = call(
        local_kernel,
        (x3, star, faces, table, flux_local, pick_local, wstiff_t),
        local_out,
        (spread,),
        4000000000,
    )

    fwd_final, adj_final, sens = call(
        last_kernel,
        (
            *received,
            pick_remote,
            gathered,
            faces,
            face_kind,
            orientation,
            worient,
            flux_sum,
            flux_neighbor,
            wlift,
            volume,
            base,
            cluster,
            sens,
        ),
        (
            pltpu.HBM(fwd_dofs.shape, F32),
            pltpu.HBM(adj_dofs.shape, F32),
            pltpu.HBM((1, ELEMS), F32),
        ),
        (keep(2, QUANT, BASIS, ELEMS), pltpu.SemaphoreType.DMA((3,))) + remote_scratch,
        4000000000,
        out_spaces={0: away, 1: away, 2: away},
    )
    return (
        jnp.transpose(fwd_final, (1, 0, 2)),
        jnp.transpose(adj_final, (1, 0, 2)),
        sens.reshape(ELEMS),
    )


def solution(mesh):
    return jax.shard_map(
        shards,
        mesh=mesh,
        in_specs=(
            P(None, None, "dom"),
            P(None, None, "dom"),
            P(None, None, None, "dom"),
            P(None, None, None, "dom"),
            P(None, None, None, "dom"),
            P("dom"),
            P("dom"),
            P(None, "dom"),
            P(None, "dom"),
            P(None, "dom"),
            P(None, "dom"),
            P(None, "dom"),
            P(None, "dom"),
            P(),
            P(),
            P(),
            P(),
        ),
        out_specs=(P(None, None, "dom"), P(None, None, "dom"), P("dom")),
        check_vma=False,
    )
```

```python
import math

import jax
import jax.numpy as jnp
from jax import lax
from jax.experimental import pallas as pl
from jax.experimental.pallas import tpu as pltpu
from jax.sharding import PartitionSpec as P

BASIS = 35
FACE_BASIS = 15
QUANT = 9
ORDER = 5
ROWS = 40
PACK = 48
FROWS = 16
ELEMS = 256
SLOTS = 64
HALF = 128
TABLE = QUANT * FROWS
MIRRORED = (0, 3, 5)
F32 = jnp.float32
BF16 = jnp.bfloat16
VMEM_LIMIT = 16 * 1024 * 1024


def dot(a, b):
    return jnp.dot(a, b, preferred_element_type=F32)


def split(x):
    hi = x.astype(BF16)
    return hi, (x - hi.astype(F32)).astype(BF16)


def spread_columns(rows, cols, starts):
    gap = lax.broadcasted_iota(jnp.int32, (rows, cols), 1) - lax.broadcasted_iota(
        jnp.int32, (rows, cols), 0
    )
    mask = gap == starts[0]
    for start in starts[1:]:
        mask = mask | (gap == start)
    return jnp.where(mask, 1.0, 0.0).astype(BF16)


def fill(out, stage, mats, step, period):
    rows, cols = out.shape
    stage[...] = jnp.zeros(stage.shape, F32)
    for k, mat in enumerate(mats):
        stage[k * step : k * step + mat.shape[0], 0 : mat.shape[1]] = mat
    hi, lo = split(stage[0:rows, :])
    width = stage.shape[1]
    out[...] = (
        dot(hi, spread_columns(width, cols, (0, period)))
        + dot(lo, spread_columns(width, cols, (2 * period,)))
    ).astype(BF16)


def fill_lift(out, face_lift):
    total = None
    for f in range(4):
        hi, lo = split(face_lift[:, f, :].T)
        base = f * FROWS
        part = dot(
            hi, spread_columns(FACE_BASIS, 12 * FROWS, (base, 4 * FROWS + base))
        ) + dot(lo, spread_columns(FACE_BASIS, 12 * FROWS, (8 * FROWS + base,)))
        total = part if total is None else total + part
    out[...] = jnp.concatenate([total, jnp.zeros((ROWS - BASIS, 12 * FROWS), F32)], 0).astype(BF16)


def stack_split(x3, q, x):
    hi, lo = split(jnp.concatenate([x, jnp.zeros((PACK - ROWS, x.shape[1]), F32)], 0))
    x3[q, 0:PACK, :] = hi
    x3[q, PACK : 2 * PACK, :] = lo
    x3[q, 2 * PACK : 3 * PACK, :] = hi


def stack_pair(x3, q, x):
    hi, lo = split(jnp.concatenate([x, jnp.zeros((PACK - ROWS, HALF), F32)], 0))
    lanes = slice(q % 2 * HALF, q % 2 * HALF + HALF)
    x3[q // 2, 0:PACK, lanes] = hi
    x3[q // 2, PACK : 2 * PACK, lanes] = lo
    x3[q // 2, 2 * PACK : 3 * PACK, lanes] = hi


def star_apply(spread, star, adjoint, half, emit):
    lanes = slice(half * HALF, half * HALF + HALF)
    acc = [None] * QUANT
    for p in range(QUANT):
        for d in range(3):
            value = spread[p, d * ROWS : d * ROWS + ROWS, lanes]
            for q in range(QUANT):
                if adjoint:
                    weight = star[p, q, d : d + 1, lanes]
                else:
                    weight = star[q, p, d : d + 1, lanes]
                term = value * weight
                acc[q] = term if acc[q] is None else acc[q] + term
    for q in range(QUANT):
        emit(q, lanes, acc[q])


def project(x3, wproj, table, n, faces=None):
    for q in range(QUANT):
        value = dot(wproj[...], x3[q])
        if faces is not None:
            faces[n, q] = value
        hi, lo = split(value)
        for f in range(4):
            lanes = slice(f * ELEMS, f * ELEMS + ELEMS)
            rows = slice(f * FROWS, f * FROWS + FROWS)
            base = n * 2 * TABLE + q * FROWS
            table[base : base + FROWS, lanes] = hi[rows]
            table[base + TABLE : base + TABLE + FROWS, lanes] = lo[rows]


def pack_send(table, pick, emit):
    found = dot(table[...], pick[...])
    low = lax.broadcasted_iota(jnp.int32, (TABLE, HALF), 1) < SLOTS
    sides = [
        found[n * 2 * TABLE : n * 2 * TABLE + TABLE]
        + found[n * 2 * TABLE + TABLE : n * 2 * TABLE + 2 * TABLE]
        for n in range(2)
    ]
    for pair in range(2):
        lanes = slice(pair * HALF, pair * HALF + HALF)
        first = sides[0][:, lanes]
        second = sides[1][:, lanes]
        emit(2 * pair, jnp.where(low, first, pltpu.roll(second, SLOTS, 1)))
        emit(2 * pair + 1, jnp.where(low, pltpu.roll(first, SLOTS, 1), second))


def unpack_received(groups, table):
    low = lax.broadcasted_iota(jnp.int32, (TABLE, HALF), 1) < SLOTS
    for pair in range(2):
        lanes = slice(pair * HALF, pair * HALF + HALF)
        first = groups[2 * pair]
        second = groups[2 * pair + 1]
        for n, value in enumerate(
            (
                jnp.where(low, first, pltpu.roll(second, SLOTS, 1)),
                jnp.where(low, pltpu.roll(first, SLOTS, 1), second),
            )
        ):
            hi, lo = split(value)
            table[n * 2 * TABLE : n * 2 * TABLE + TABLE, lanes] = hi
            table[n * 2 * TABLE + TABLE : n * 2 * TABLE + 2 * TABLE, lanes] = lo


def one_hot(codes, first, rows):
    ids = lax.broadcasted_iota(jnp.int32, (rows, codes.shape[1]), 0) + first
    return jnp.where(ids == codes, 1.0, 0.0).astype(BF16)


def least_kernel(timescale, halves):
    least = jnp.minimum(timescale[:, 0:HALF], timescale[:, HALF:])
    halves[...] = jnp.broadcast_to(least, halves.shape)


def first_kernel(
    fwd,
    adj,
    star,
    stiffness,
    face_proj,
    send_element,
    send_face,
    face_kind,
    neighbor_index,
    neighbor_face,
    cluster,
    orientation,
    face_lift,
    face_orient,
    flux_local,
    derived,
    last,
    pick_local,
    pick_remote,
    pick_send,
    take_fine,
    give_fine,
    fine_star,
    wstiff,
    wstiff_t,
    wproj,
    wlift,
    worient,
    star_kept,
    local_kept,
    kind_kept,
    turn_kept,
    cluster_kept,
    stage,
    x3,
    spread,
    codes,
    series,
    raw,
    local_picks,
    star_rows,
    found,
    sems,
):
    copies = [
        pltpu.make_async_copy(source, kept, sems.at[2, i])
        for i, (source, kept) in enumerate(
            ((star, star_kept), (flux_local, local_kept))
        )
    ]
    loads = [
        pltpu.make_async_copy(field, raw.at[n], sems.at[3, n]) for n, field in enumerate((fwd, adj))
    ]
    for copy in loads + copies:
        copy.start()
    star = star_kept
    kind_kept[...] = face_kind[...]
    turn_kept[...] = orientation[...]
    cluster_kept[...] = cluster[...]
    fill(wstiff, stage.at[0], [stiffness[d] for d in range(3)], ROWS, PACK)
    fill(wstiff_t, stage.at[1], [stiffness[d].T for d in range(3)], ROWS, PACK)
    fill(wproj, stage.at[2], [face_proj[:, f, :] for f in range(4)], FROWS, PACK)
    fill(worient, stage.at[3], [face_orient[o] for o in range(3)], FROWS, FROWS)
    fill_lift(wlift, face_lift)

    send_code = send_face[...] * ELEMS + send_element[...]
    for g in range(4):
        codes[0:1, g * SLOTS : g * SLOTS + SLOTS] = send_code[g : g + 1]
    for block in range(4):
        rows = slice(block * ELEMS, block * ELEMS + ELEMS)
        pick_send[rows, :] = one_hot(codes[0:1, :], block * ELEMS, ELEMS)
    for f in range(4):
        lanes = slice(f * ELEMS, f * ELEMS + ELEMS)
        kind = face_kind[f : f + 1, :]
        index = neighbor_index[f : f + 1, :]
        local = jnp.where(kind == 0, neighbor_face[f : f + 1, :] * ELEMS + index, -1)
        remote = jnp.where(kind == 1, index, -1)
        for block in range(4):
            rows = slice(block * ELEMS, block * ELEMS + ELEMS)
            local_picks[rows, lanes] = one_hot(local, block * ELEMS, ELEMS)
        pick_remote[:, lanes] = one_hot(remote, 0, ELEMS)
    table_out = pltpu.make_async_copy(local_picks, pick_local, sems.at[3, 2])
    table_out.start()

    fine = cluster[...] == 0
    upper = lax.broadcasted_iota(jnp.int32, (ELEMS, ELEMS), 0) < lax.broadcasted_iota(
        jnp.int32, (ELEMS, ELEMS), 1
    )
    flags = jnp.broadcast_to(jnp.where(fine, 1.0, 0.0), (FROWS, ELEMS)).astype(BF16)
    rank = dot(flags, jnp.where(upper, 1.0, 0.0).astype(BF16))[0:1]
    place_of = jnp.where(fine, rank.astype(jnp.int32), -1)
    slot = lax.broadcasted_iota(jnp.int32, (HALF, ELEMS), 0)
    slot = jnp.where(slot < SLOTS, slot, slot - SLOTS)
    chosen = jnp.where(slot == place_of, 1.0, 0.0)
    below = lax.broadcasted_iota(jnp.int32, (HALF, ELEMS), 0) < SLOTS
    for n in range(2):
        own = jnp.where(below, chosen, 0.0) if n == 0 else jnp.where(below, 0.0, chosen)
        give_fine[n] = own.astype(BF16)
        take_fine[n] = own.T.astype(BF16)
    copies[0].wait()
    for q in range(QUANT):
        for p in range(QUANT):
            base = 4 * (q * QUANT + p)
            star_rows[base : base + 3, :] = star[q, p]
    hi, lo = split(star_rows[...])
    take = chosen.T.astype(BF16)
    found[...] = dot(hi, take) + dot(lo, take)
    low1 = lax.broadcasted_iota(jnp.int32, (3, HALF), 1) < SLOTS
    for q in range(QUANT):
        for p in range(QUANT):
            plain = 4 * (q * QUANT + p)
            swapped = 4 * (p * QUANT + q)
            fine_star[q, p] = jnp.where(
                low1, found[plain : plain + 3, :], found[swapped : swapped + 3, :]
            )

    for n in range(2):
        loads[n].wait()
        for q in range(QUANT):
            series[0, n, q, 0:BASIS, :] = raw[n, q]
            series[0, n, q, BASIS:ROWS, :] = jnp.zeros((ROWS - BASIS, ELEMS), F32)

    def step(degree, write):
        for n in range(2):
            for q in range(QUANT):
                stack_split(x3, q, series[degree, n, q])
            for q in range(QUANT):
                spread[q] = dot(wstiff[...], x3[q])
            for half in range(2):

                def emit(q, lanes, value):
                    write(n, q, lanes, value)

                star_apply(spread, star, n == 1, half, emit)

    def stored(degree, n):
        return pltpu.make_async_copy(
            series.at[degree + 1, n], derived.at[n, degree], sems.at[n, degree]
        )

    def early_step(degree, _):
        def write(n, q, lanes, value):
            series[degree + 1, n, q, :, lanes] = value

        step(degree, write)
        for n in range(2):
            stored(degree, n).start()
        return 0

    def write_last(n, q, lanes, value):
        last[n, q, :, lanes] = value

    lax.fori_loop(0, ORDER - 2, early_step, 0)
    step(ORDER - 2, write_last)
    copies[1].wait()
    table_out.wait()
    for n in range(2):
        for degree in range(ORDER - 2):
            stored(degree, n).wait()


def weights_of(smallest):
    dt = 0.5 * smallest
    early = []
    late = []
    power = dt
    for degree in range(ORDER):
        scale = 1.0 / math.factorial(degree + 1)
        early.append(power * scale)
        late.append(power * (scale * (2.0 ** (degree + 1) - 1.0)))
        power = power * dt
    return early, late


def integral_kernel(
    steps,
    fwd,
    adj,
    derived,
    last,
    pick_send,
    wproj,
    flux_neighbor,
    out0,
    out1,
    out2,
    out3,
    integral,
    faces,
    table,
    x3,
    series,
    start,
    least,
    neighbor_kept,
    sems,
):
    outs = (out0, out1, out2, out3)
    third = QUANT // 3
    starts = []
    copies = []
    for n, field in enumerate((fwd, adj)):
        starts.append(pltpu.make_async_copy(field, start.at[n], sems.at[n, 3]))
        starts[n].start()
        copies.append([])
        for part in range(3):
            some = slice(part * third, part * third + third)
            copies[n].append(
                pltpu.make_async_copy(
                    derived.at[n, :, some], series.at[n, :, some], sems.at[n, part]
                )
            )
            copies[n][part].start()
    keeping = pltpu.make_async_copy(flux_neighbor, neighbor_kept, sems.at[2, 0])
    keeping.start()
    smallest = jnp.min(steps[...])
    least[...] = jnp.full(least.shape, smallest, F32)
    early, _ = weights_of(smallest)
    for n in range(2):
        starts[n].wait()
        for q in range(QUANT):
            if q % third == 0:
                copies[n][q // third].wait()
            integral[n, q, 0:BASIS, :] = early[0] * start[n, q]
            integral[n, q, BASIS:ROWS, :] = jnp.zeros((ROWS - BASIS, ELEMS), F32)
            total = integral[n, q] + early[ORDER - 1] * last[n, q]
            for degree in range(1, ORDER - 1):
                total = total + early[degree] * series[n, degree - 1, q]
            integral[n, q] = total
            stack_split(x3.at[n], q, total)
        project(x3.at[n], wproj, table, n, faces)

    def send(g, value):
        outs[g][...] = value

    pack_send(table, pick_send, send)
    keeping.wait()


def flux_apply(source, weights, adjoint, n, f, half, acc):
    lanes = slice(half * HALF, half * HALF + HALF)
    rows = slice(f * FROWS, f * FROWS + FROWS)
    for p in range(QUANT):
        value = source[n, p, rows, lanes]
        for q in range(QUANT):
            if adjoint:
                weight = weights[p, q, f : f + 1, lanes]
            else:
                weight = weights[q, p, f : f + 1, lanes]
            term = value * weight
            acc[q] = term if acc[q] is None else acc[q] + term
    return acc


def local_part(
    x3, wstiff_t, spread, star, faces, table, flux_local, pick_local, volume, flux_sum, gathered
):
    for n in range(2):
        for q in range(QUANT):
            spread[q] = dot(wstiff_t[...], x3[n, q])
        for half in range(2):

            def emit(q, lanes, value):
                volume[n, q, :, lanes] = value

            star_apply(spread, star, n == 1, half, emit)
    for f in range(4):
        lanes = slice(f * ELEMS, f * ELEMS + ELEMS)
        found = dot(table[...], pick_local[:, lanes])
        for n in range(2):
            gathered[n, f] = (
                found[n * 2 * TABLE : n * 2 * TABLE + TABLE]
                + found[n * 2 * TABLE + TABLE : n * 2 * TABLE + 2 * TABLE]
            )
    for n in range(2):
        for f in range(4):
            for half in range(2):
                acc = flux_apply(faces, flux_local, n == 1, n, f, half, [None] * QUANT)
                for q in range(QUANT):
                    flux_sum[
                        n,
                        q,
                        f * FROWS : f * FROWS + FROWS,
                        half * HALF : half * HALF + HALF,
                    ] = acc[q]


def remote_part(
    groups,
    rtable,
    pick_remote,
    gathered,
    faces,
    face_kind,
    orientation,
    worient,
    x3o,
    other,
    flux_sum,
    flux_neighbor,
    x3l,
    wlift,
    volume,
    emit,
):
    unpack_received(groups, rtable)
    for f in range(4):
        lanes = slice(f * ELEMS, f * ELEMS + ELEMS)
        rows = slice(f * FROWS, f * FROWS + FROWS)
        found = dot(rtable[...], pick_remote[:, lanes])
        turn = jnp.broadcast_to(orientation[f : f + 1, :], (FROWS, ELEMS))
        unturned = turn == 0
        turned_once = turn == 1
        mirror = jnp.broadcast_to(
            jnp.where(face_kind[f : f + 1, :] == 2, 1.0, 0.0), (FROWS, ELEMS)
        )
        for n in range(2):
            total = (
                found[n * 2 * TABLE : n * 2 * TABLE + TABLE]
                + found[n * 2 * TABLE + TABLE : n * 2 * TABLE + 2 * TABLE]
                + gathered[n, f]
            )
            hi, lo = split(total)
            for q in range(QUANT):
                part = slice(q * FROWS, q * FROWS + FROWS)
                x3o[n, f, q, 0:FROWS, :] = hi[part]
                x3o[n, f, q, FROWS : 2 * FROWS, :] = lo[part]
                x3o[n, f, q, 2 * FROWS : 3 * FROWS, :] = hi[part]
            for q in range(QUANT):
                three = dot(worient[...], x3o[n, f, q])
                turned = jnp.where(
                    unturned,
                    three[0:FROWS],
                    jnp.where(turned_once, three[FROWS : 2 * FROWS], three[2 * FROWS : 3 * FROWS]),
                )
                own = faces[n, q, rows, :] * mirror
                other[n, q, rows, :] = turned - own if q in MIRRORED else turned + own
    for n in range(2):
        for f in range(4):
            rows = slice(f * FROWS, f * FROWS + FROWS)
            for half in range(2):
                lanes = slice(half * HALF, half * HALF + HALF)
                acc = [flux_sum[n, q, rows, lanes] for q in range(QUANT)]
                acc = flux_apply(other, flux_neighbor, n == 1, n, f, half, acc)
                for q in range(QUANT):
                    hi, lo = split(acc[q])
                    x3l[q, f * FROWS : f * FROWS + FROWS, lanes] = hi
                    x3l[q, (4 + f) * FROWS : (5 + f) * FROWS, lanes] = lo
                    x3l[q, (8 + f) * FROWS : (9 + f) * FROWS, lanes] = hi
        for q in range(QUANT):
            emit(n, q, volume[n, q] + dot(wlift[...], x3l[q]))


def middle_kernel(
    least,
    start,
    integral,
    later,
    in0,
    in1,
    in2,
    in3,
    pick_remote,
    pick_send,
    take_fine,
    give_fine,
    fine_star,
    gathered,
    faces,
    face_kind,
    orientation,
    worient,
    flux_sum,
    flux_neighbor,
    wlift,
    volume,
    cluster,
    wstiff,
    wproj,
    out0,
    out1,
    out2,
    out3,
    base,
    faces_out,
    table,
    x3,
    sens,
    rtable,
    x3o,
    other,
    x3l,
    wide,
    x3c,
    spread_c,
    fields_c,
):
    outs = (out0, out1, out2, out3)
    early, _ = weights_of(jnp.min(least[...]))
    x3c[QUANT // 2, :, HALF:] = jnp.zeros((3 * PACK, HALF), BF16)
    fine = jnp.broadcast_to(cluster[...], (ROWS, ELEMS)) == 0
    active = jnp.broadcast_to(cluster[...], (ROWS, ELEMS)) <= 1

    def emit_first(n, q, value):
        before = jnp.concatenate([start[n, q], jnp.zeros((ROWS - BASIS, ELEMS), F32)], 0)
        moved = before + value
        base[n, q] = jnp.where(active, moved, before)
        hi, lo = split(jnp.concatenate([moved, jnp.zeros((PACK - ROWS, ELEMS), F32)], 0))
        wide[q, :, 2 * n * ELEMS : (2 * n + 1) * ELEMS] = hi
        wide[q, :, (2 * n + 1) * ELEMS : (2 * n + 2) * ELEMS] = lo

    remote_part(
        [in0[...], in1[...], in2[...], in3[...]],
        rtable,
        pick_remote,
        gathered,
        faces,
        face_kind,
        orientation,
        worient,
        x3o,
        other,
        flux_sum,
        flux_neighbor,
        x3l,
        wlift,
        volume,
        emit_first,
    )

    for q in range(QUANT):
        value = jnp.zeros((ROWS, HALF), F32)
        for n in range(2):
            for part in range(2):
                lanes = slice((2 * n + part) * ELEMS, (2 * n + part + 1) * ELEMS)
                value = value + dot(wide[q, :, lanes], take_fine[n])[0:ROWS]
        fields_c[q] = early[0] * value
        stack_pair(x3c, q, value)
    for degree in range(1, ORDER):
        for pair in range((QUANT + 1) // 2):
            spread_c[pair] = dot(wstiff[...], x3c[pair])
        acc = [None] * QUANT
        for p in range(QUANT):
            side = slice(p % 2 * HALF, p % 2 * HALF + HALF)
            for d in range(3):
                value = spread_c[p // 2, d * ROWS : d * ROWS + ROWS, side]
                for q in range(QUANT):
                    term = value * fine_star[q, p, d : d + 1, :]
                    acc[q] = term if acc[q] is None else acc[q] + term
        for q in range(QUANT):
            fields_c[q] = fields_c[q] + early[degree] * acc[q]
            if degree < ORDER - 1:
                stack_pair(x3c, q, acc[q])

    products = jnp.zeros((ROWS, ELEMS), F32)
    for q in range(QUANT):
        hi, lo = split(jnp.concatenate([fields_c[q], jnp.zeros((PACK - ROWS, HALF), F32)], 0))
        both = []
        for n in range(2):
            renewed = (dot(hi, give_fine[n]) + dot(lo, give_fine[n]))[0:ROWS]
            value = jnp.where(fine, renewed, later[n, q])
            stack_split(x3.at[n], q, value)
            both.append(value)
        products = products + integral[0, q] * integral[1, q] + both[0] * both[1]
    sens[...] = jnp.sum(products, axis=0, keepdims=True)
    for n in range(2):
        project(x3.at[n], wproj, table, n, faces_out)

    def send(g, value):
        outs[g][...] = value

    pack_send(table, pick_send, send)


def local_kernel(
    x3, star, faces, table, flux_local, pick_local, wstiff_t, volume, flux_sum, gathered, spread
):
    local_part(
        x3, wstiff_t, spread, star, faces, table, flux_local, pick_local, volume, flux_sum, gathered
    )


def first_local_kernel(
    x3,
    star,
    faces,
    table,
    flux_local,
    pick_local,
    wstiff_t,
    least,
    start,
    series,
    last,
    volume,
    flux_sum,
    gathered,
    later,
    spread,
):
    local_part(
        x3, wstiff_t, spread, star, faces, table, flux_local, pick_local, volume, flux_sum, gathered
    )
    _, late = weights_of(jnp.min(least[...]))
    for n in range(2):
        for q in range(QUANT):
            later[n, q, 0:BASIS, :] = late[0] * start[n, q]
            later[n, q, BASIS:ROWS, :] = jnp.zeros((ROWS - BASIS, ELEMS), F32)
            total = later[n, q] + late[ORDER - 1] * last[n, q]
            for degree in range(1, ORDER - 1):
                total = total + late[degree] * series[n, degree - 1, q]
            later[n, q] = total


def last_kernel(
    in0,
    in1,
    in2,
    in3,
    pick_remote,
    gathered,
    faces,
    face_kind,
    orientation,
    worient,
    flux_sum,
    flux_neighbor,
    wlift,
    volume,
    base,
    cluster,
    sens,
    fwd,
    adj,
    sens_out,
    final,
    sems,
    rtable,
    x3o,
    other,
    x3l,
):
    active = jnp.broadcast_to(cluster[...], (ROWS, ELEMS)) <= 1
    copies = [
        pltpu.make_async_copy(final.at[n], out, sems.at[n]) for n, out in enumerate((fwd, adj))
    ]
    copies.append(pltpu.make_async_copy(sens, sens_out, sems.at[2]))
    copies[2].start()

    def emit(n, q, value):
        done = base[n, q] + jnp.where(active, value, 0.0)
        final[n, q] = done[0:BASIS]
        if q == QUANT - 1:
            copies[n].start()

    remote_part(
        [in0[...], in1[...], in2[...], in3[...]],
        rtable,
        pick_remote,
        gathered,
        faces,
        face_kind,
        orientation,
        worient,
        x3o,
        other,
        flux_sum,
        flux_neighbor,
        x3l,
        wlift,
        volume,
        emit,
    )
    for copy in copies:
        copy.wait()


def call(kernel, args, outs, scratch, flops, spaces=None, out_spaces=None, far=()):
    whole = pl.BlockSpec(memory_space=pltpu.VMEM)
    spaces = spaces or {}
    out_spaces = out_spaces or {}
    args = [
        pltpu.with_memory_space_constraint(x, pltpu.HBM if i in far else pltpu.VMEM)
        for i, x in enumerate(args)
    ]
    return pl.pallas_call(
        kernel,
        out_shape=outs,
        in_specs=[spaces.get(i, whole) for i in range(len(args))],
        out_specs=tuple(out_spaces.get(i, whole) for i in range(len(outs))),
        scratch_shapes=scratch,
        compiler_params=pltpu.CompilerParams(vmem_limit_bytes=VMEM_LIMIT),
        cost_estimate=pl.CostEstimate(flops=flops, bytes_accessed=4000000, transcendentals=0),
    )(*args)


def keep(*shape, dtype=F32):
    return pltpu.VMEM(shape, dtype)


def deliver(outgoing):
    received = []
    for value, by in zip(outgoing, (2, 1, -1, -2)):
        length = lax.axis_size("dom")
        pairs = [(i, (i + by) % length) for i in range(length)]
        received.append(lax.ppermute(value, "dom", pairs))
    return received


def shards(
    fwd_dofs,
    adj_dofs,
    star,
    flux_local,
    flux_neighbor,
    timescale,
    cluster,
    face_kind,
    neighbor_index,
    neighbor_face,
    orientation,
    send_element,
    send_face,
    stiffness,
    face_proj,
    face_lift,
    face_orient,
):
    count = lax.axis_size("dom")
    (halves,) = call(
        least_kernel,
        (timescale.reshape(1, ELEMS),),
        (keep(count, HALF),),
        (),
        100000,
        far=(0,),
    )
    steps = lax.all_to_all(halves.reshape(count, 1, HALF), "dom", 0, 0)
    cluster = cluster.reshape(1, ELEMS)

    fwd_dofs = jnp.transpose(fwd_dofs, (1, 0, 2))
    adj_dofs = jnp.transpose(adj_dofs, (1, 0, 2))
    star = jnp.transpose(star, (1, 2, 0, 3))
    flux_local = jnp.transpose(flux_local, (1, 2, 0, 3))
    flux_neighbor = jnp.transpose(flux_neighbor, (1, 2, 0, 3))
    face_proj = jnp.transpose(face_proj, (1, 0, 2))
    face_lift = jnp.transpose(face_lift, (2, 0, 1))

    bf16 = {"dtype": BF16}
    whole = pl.BlockSpec(memory_space=pltpu.VMEM)
    away = pl.BlockSpec(memory_space=pl.ANY)
    message = keep(TABLE, HALF)
    face_data = keep(2, QUANT, 4 * FROWS, ELEMS)
    table_data = keep(4 * TABLE, 4 * ELEMS, **bf16)
    stacked = keep(2, QUANT, 3 * PACK, ELEMS, **bf16)
    fields = keep(2, QUANT, ROWS, ELEMS)
    apart = (2, ORDER - 2, QUANT, ROWS, ELEMS)
    spread = keep(QUANT, 3 * ROWS, ELEMS)
    remote_scratch = (
        keep(4 * TABLE, ELEMS, **bf16),
        keep(2, 4, QUANT, 3 * FROWS, ELEMS, **bf16),
        face_data,
        keep(QUANT, 12 * FROWS, ELEMS, **bf16),
    )

    (
        derived,
        last,
        pick_local,
        pick_remote,
        pick_send,
        take_fine,
        give_fine,
        fine_star,
        wstiff,
        wstiff_t,
        wproj,
        wlift,
        worient,
        star,
        flux_local,
        face_kind,
        orientation,
        cluster,
    ) = call(
        first_kernel,
        (
            fwd_dofs,
            adj_dofs,
            star,
            stiffness,
            face_proj,
            send_element,
            send_face,
            face_kind,
            neighbor_index,
            neighbor_face,
            cluster,
            orientation,
            face_lift,
            face_orient,
            flux_local,
        ),
        (
            pltpu.HBM(apart, F32),
            fields,
            pltpu.HBM((4 * ELEMS, 4 * ELEMS), BF16),
            keep(ELEMS, 4 * ELEMS, **bf16),
            keep(4 * ELEMS, ELEMS, **bf16),
            keep(2, ELEMS, HALF, **bf16),
            keep(2, HALF, ELEMS, **bf16),
            keep(QUANT, QUANT, 3, HALF),
            keep(3 * ROWS, 3 * PACK, **bf16),
            keep(3 * ROWS, 3 * PACK, **bf16),
            keep(4 * FROWS, 3 * PACK, **bf16),
            keep(ROWS, 12 * FROWS, **bf16),
            keep(3 * FROWS, 3 * FROWS, **bf16),
            keep(*star.shape),
            keep(*flux_local.shape),
            keep(4, ELEMS, dtype=jnp.int32),
            keep(4, ELEMS, dtype=jnp.int32),
            keep(1, ELEMS, dtype=jnp.int32),
        ),
        (
            keep(4, 128, 128),
            keep(QUANT, 3 * PACK, ELEMS, **bf16),
            spread,
            keep(8, ELEMS, dtype=jnp.int32),
            keep(ORDER - 1, 2, QUANT, ROWS, ELEMS),
            keep(2, QUANT, BASIS, ELEMS),
            keep(4 * ELEMS, 4 * ELEMS, **bf16),
            keep(336, ELEMS),
            keep(336, HALF),
            pltpu.SemaphoreType.DMA((4, ORDER - 1)),
        ),
        14000000000,
        far=range(15),
        spaces={0: away, 1: away, 2: away, 14: away},
        out_spaces={0: away, 2: away},
    )

    local_out = (fields, face_data, keep(2, 4, TABLE, ELEMS))
    *outgoing, integral, faces, table, x3, series, start, least, flux_neighbor = call(
        integral_kernel,
        (steps, fwd_dofs, adj_dofs, derived, last, pick_send, wproj, flux_neighbor),
        (message,) * 4
        + (
            fields,
            face_data,
            table_data,
            stacked,
            keep(*apart),
            keep(2, QUANT, BASIS, ELEMS),
            keep(8, HALF),
            keep(*flux_neighbor.shape),
        ),
        (pltpu.SemaphoreType.DMA((3, 4)),),
        2000000000,
        spaces={1: away, 2: away, 3: away, 7: away},
        far=(1, 2, 3, 7),
    )
    received = deliver(outgoing)
    volume, flux_sum, gathered, later = call(
        first_local_kernel,
        (x3, star, faces, table, flux_local, pick_local, wstiff_t, least, start, series, last),
        local_out + (fields,),
        (spread,),
        4000000000,
    )

    *outgoing, base, faces, table, x3, sens = call(
        middle_kernel,
        (
            least,
            start,
            integral,
            later,
            *received,
            pick_remote,
            pick_send,
            take_fine,
            give_fine,
            fine_star,
            gathered,
            faces,
            face_kind,
            orientation,
            worient,
            flux_sum,
            flux_neighbor,
            wlift,
            volume,
            cluster,
            wstiff,
            wproj,
        ),
        (message,) * 4
        + (keep(2, QUANT, ROWS, ELEMS), face_data, table_data, stacked, keep(1, ELEMS)),
        remote_scratch
        + (
            keep(QUANT, PACK, 4 * ELEMS, **bf16),
            keep((QUANT + 1) // 2, 3 * PACK, ELEMS, **bf16),
            keep((QUANT + 1) // 2, 3 * ROWS, ELEMS),
            keep(QUANT, ROWS, HALF),
        ),
        8000000000,
    )
    received = deliver(outgoing)
    volume, flux_sum, gathered = call(
        local_kernel,
        (x3, star, faces, table, flux_local, pick_local, wstiff_t),
        local_out,
        (spread,),
        4000000000,
    )

    fwd_final, adj_final, sens = call(
        last_kernel,
        (
            *received,
            pick_remote,
            gathered,
            faces,
            face_kind,
            orientation,
            worient,
            flux_sum,
            flux_neighbor,
            wlift,
            volume,
            base,
            cluster,
            sens,
        ),
        (
            pltpu.HBM(fwd_dofs.shape, F32),
            pltpu.HBM(adj_dofs.shape, F32),
            pltpu.HBM((1, ELEMS), F32),
        ),
        (keep(2, QUANT, BASIS, ELEMS), pltpu.SemaphoreType.DMA((3,))) + remote_scratch,
        4000000000,
        out_spaces={0: away, 1: away, 2: away},
    )
    return (
        jnp.transpose(fwd_final, (1, 0, 2)),
        jnp.transpose(adj_final, (1, 0, 2)),
        sens.reshape(ELEMS),
    )


def solution(mesh):
    return jax.shard_map(
        shards,
        mesh=mesh,
        in_specs=(
            P(None, None, "dom"),
            P(None, None, "dom"),
            P(None, None, None, "dom"),
            P(None, None, None, "dom"),
            P(None, None, None, "dom"),
            P("dom"),
            P("dom"),
            P(None, "dom"),
            P(None, "dom"),
            P(None, "dom"),
            P(None, "dom"),
            P(None, "dom"),
            P(None, "dom"),
            P(),
            P(),
            P(),
            P(),
        ),
        out_specs=(P(None, None, "dom"), P(None, None, "dom"), P("dom")),
        check_vma=False,
    )
```
